768 devices in a mesh: grp: 64 (over x, y, core), sub: 12 (over z).
Axes of the slice: x: 4, y: 8, z: 12, core: 2. Of those that a mesh axis runs over, the one named last changes fastest.
Arguments:
- tokens: bfloat16 [3072, 32, 256], P(('grp', 'sub')), may hold values from -64 to 64
- proj_weight: bfloat16 [256, 256], replicated, may hold values from -2 to 2
- match_grad: bfloat16 [98304, 1024], P(('grp', 'sub')), may hold values from -3072 to 3072
- edge_first: int32 [98304], P(('grp', 'sub')), may hold values from 0 to 47, as said below
- pair_second_image: int32 [98304], P(('grp', 'sub')), may hold values from 0 to 63, as said below
- send_pick: int32 [49152], P(('grp', 'sub')), may hold values from 0 to 3, as said below
Outputs:
- token_grad: bfloat16 [3072, 32, 256], P(('grp', 'sub'))
The draws below stay inside these ranges and needn't reach their ends.
Inputs may be any that keep to these rules, and one draw needn't show every extreme that they name: On each device the pairs (edge_first, pair_second_image) are distinct. `pair_second_image`: on each device every receive slot 0 to 63 is named by at least one pair. `send_pick`: for each device and each index p of grp, the 1 entries of its send slots p * 1 to p + 1 - 1 name different images.
All inputs are finite; a program needn't handle non-finite values.
Results may differ from the reference program's by a relative error of at most 0.017.
Values may be sent and summed in bfloat16 or wider, within the bound.
A program may use at most 64 MiB of HBM per device.

```python
import math
import jax
import jax.numpy as jnp
from jax import lax

D = 256
L = 32
IMG_DEV = 4
EDGE_DEV = 128
SLOTS = 1
RECV = 64
GROUP_IMG = 48
IMAGES = 3072
EDGES = 98304
SENDS = 49152
N_GRP = 64
N_SUB = 12


def feature_levels(key):
    return jax.random.uniform(jax.random.fold_in(key, 17), (D,), jnp.float32, 0.0, 1.0)


def draw_tokens(key, part):
    random_key_root, key_row = jax.random.split(jax.random.fold_in(key, 7), 2)
    level = feature_levels(key)
    diag_size = 1.0 - 0.4 * level
    base = jnp.clip(jax.random.normal(random_key_root, (IMAGES, L, D), jnp.float32), -4.0, 4.0)
    row_scale = jnp.exp(jax.random.uniform(key_row, (IMAGES, L, 1), jnp.float32, 0.0, math.log(10.0)))
    col_scale = 0.06 * jnp.exp(level * math.log(10.0)) / diag_size
    return jnp.clip(base * row_scale * col_scale[None, None, :], -64.0, 64.0).astype(jnp.bfloat16)


def draw_proj_weight(key, part):
    key_sign, key_off = jax.random.split(jax.random.fold_in(key, 3))
    level = feature_levels(key)
    diag_size = 1.0 - 0.4 * level
    signs = jnp.where(jax.random.randint(key_sign, (D,), 0, 2, dtype=jnp.int32) == 1, 1.0, -1.0).astype(jnp.float32)
    off_diag = jnp.clip(jax.random.normal(key_off, (D, D), jnp.float32), -4.0, 4.0) * (0.3 / math.sqrt(D))
    index = jnp.arange(D, dtype=jnp.int32)
    on_diag = index[:, None] == index[None, :]
    weight = jnp.where(on_diag, (signs * diag_size)[None, :], off_diag)
    return jnp.clip(weight, -2.0, 2.0).astype(jnp.bfloat16)


def edge_table(key):
    base_key = jax.random.fold_in(key, 11)
    pair_count = GROUP_IMG * RECV

    def one_block(block_index):
        block_key = jax.random.fold_in(base_key, block_index)
        key_noise, key_hub, key_anchor = jax.random.split(block_key, 3)
        noise = jax.random.randint(key_noise, (GROUP_IMG, RECV), 0, 1024, dtype=jnp.int32)
        hub = jax.random.randint(key_hub, (1, RECV), 0, 4, dtype=jnp.int32) * 1024
        anchor_row = jax.random.randint(key_anchor, (RECV,), 0, GROUP_IMG, dtype=jnp.int32)
        anchor = (jnp.arange(GROUP_IMG, dtype=jnp.int32)[:, None] == anchor_row[None, :]).astype(jnp.int32) * 8192
        score = (noise + hub + anchor).reshape(pair_count) * pair_count + jnp.arange(pair_count, dtype=jnp.int32)
        _, picked = lax.top_k(score, EDGE_DEV)
        picked = picked.astype(jnp.int32)
        return (picked // RECV, picked % RECV)
    first_images, seconds = lax.map(one_block, jnp.arange(EDGES // EDGE_DEV, dtype=jnp.int32))
    return (first_images.reshape(EDGES).astype(jnp.int32), seconds.reshape(EDGES).astype(jnp.int32))


def draw_edge_first(key, part):
    return edge_table(key)[0]


def draw_pair_second_image(key, part):
    return edge_table(key)[1]


def draw_send_pick(key, part):
    keys = jax.random.split(jax.random.fold_in(key, 5), SENDS // SLOTS)

    def one_peer(peer_key):
        return jax.random.permutation(peer_key, IMG_DEV)[:SLOTS].astype(jnp.int32)
    return jax.vmap(one_peer)(keys).reshape(SENDS).astype(jnp.int32)


def block_levels(rng, dims, cuts, least, top_value):
    def one(axis_at, blocks):
        heights = jax.random.uniform(jax.random.fold_in(jax.random.fold_in(rng, 6), axis_at), (blocks,), jnp.float32, least / len(cuts), top_value / len(cuts))
        return jnp.repeat(jnp.exp(heights), dims[axis_at] // blocks).reshape((-1,) + (1,) * (len(dims) - axis_at - 1))

    factor_of = one(*cuts[0])
    for cut in cuts[1:]:
        factor_of = factor_of * one(*cut)
    return factor_of


def gaussian(key, extent, deviation, bound, pieces=(), kind=jnp.bfloat16):
    array = jax.random.normal(key, extent, jnp.float32) * deviation
    if len(pieces) > 0:
        array = block_levels(key, extent, pieces, -0.22, 0.18) * array
    return jnp.clip(array, min=-bound, max=bound).astype(kind)


def setup_inputs(seed: int = 0) -> dict:
    key_of = jax.random.split(jax.random.key(seed), 7)
    return {
        "tokens": draw_tokens(jax.random.fold_in(key_of[6], 71), 0),
        "proj_weight": draw_proj_weight(jax.random.fold_in(key_of[6], 71), 0),
        "match_grad": gaussian(key_of[2], (EDGES, L * L), 512.0, 3072.0, ((0, 768),)),
        "edge_first": draw_edge_first(jax.random.fold_in(key_of[6], 71), 0),
        "pair_second_image": draw_pair_second_image(jax.random.fold_in(key_of[6], 71), 0),
        "send_pick": draw_send_pick(jax.random.fold_in(key_of[6], 71), 0),
    }


EPSILON = 1e-05
SOFTMAX_COOLING = 0.1

def normalize(tokens_flat, proj_weight):
    feature = jnp.dot(tokens_flat, proj_weight, preferred_element_type=jnp.float32)
    inv_rms = lax.rsqrt(lax.optimization_barrier(jnp.mean(feature * feature, axis=-1, keepdims=True)) + EPSILON)
    return (feature * inv_rms, inv_rms)

def edge_terms(first_image_features, second_feats, match_block):
    score_scale = 1.0 / (first_image_features.shape[-1] * SOFTMAX_COOLING)
    first_wide = first_image_features.astype(jnp.float32)
    second_wide = second_feats.astype(jnp.float32)
    scores = jnp.einsum('eid,ejd->eij', first_wide, second_wide) * score_scale
    expo = jnp.exp(scores)
    rows = expo / lax.optimization_barrier(jnp.sum(expo, axis=2, keepdims=True))
    cols = expo / lax.optimization_barrier(jnp.sum(expo, axis=1, keepdims=True))
    incoming_gradient = match_block.astype(jnp.float32)
    d_rows = incoming_gradient * cols
    d_cols = incoming_gradient * rows
    d_scores = rows * (d_rows - lax.optimization_barrier(jnp.sum(d_rows * rows, axis=2, keepdims=True))) + cols * (d_cols - lax.optimization_barrier(jnp.sum(d_cols * cols, axis=1, keepdims=True)))
    d_scaled = lax.optimization_barrier((d_scores * score_scale).astype(jnp.bfloat16)).astype(jnp.float32)
    grad_first = jnp.einsum('eij,ejd->eid', d_scaled, second_wide)
    grad_second = jnp.einsum('eij,eid->ejd', d_scaled, first_wide)
    return (grad_first, grad_second)

def reference(tokens, proj_weight, match_grad, edge_first, pair_second_image, send_pick):
    images = tokens.shape[0]
    normed, inv_rms = normalize(tokens.reshape(images * L, D), proj_weight)
    normed_b = normed.astype(jnp.bfloat16).reshape(images, L, D)
    devices = N_GRP * N_SUB
    picks_all = send_pick.reshape(devices, RECV)
    grads_all = match_grad.reshape(devices, EDGE_DEV, L, L)
    firsts_all = edge_first.reshape(devices, EDGE_DEV)
    seconds_all = pair_second_image.reshape(devices, EDGE_DEV)
    slot_ids = jnp.arange(RECV, dtype=jnp.int32)

    def device_step(total, inputs):
        device, grads, first_images, seconds = inputs
        group = device // N_SUB
        member = device % N_SUB
        pool = lax.dynamic_slice_in_dim(normed_b, (group * GROUP_IMG).astype(jnp.int32), GROUP_IMG, 0)
        senders = slot_ids // SLOTS * N_SUB + member
        picked = picks_all[senders, group * SLOTS + slot_ids % SLOTS]
        slot_images = (senders * IMG_DEV + picked).astype(jnp.int32)
        received = normed_b[slot_images]
        grad_first, grad_second = edge_terms(pool[first_images], received[seconds], grads)
        pool_part = jax.ops.segment_sum(grad_first, first_images, num_segments=GROUP_IMG)
        slot_part = jax.ops.segment_sum(grad_second, seconds, num_segments=RECV)
        pool_round = lax.optimization_barrier(pool_part.astype(jnp.bfloat16)).astype(jnp.float32)
        slot_round = lax.optimization_barrier(slot_part.astype(jnp.bfloat16)).astype(jnp.float32)
        start = (group * GROUP_IMG).astype(jnp.int32)
        block = lax.dynamic_slice_in_dim(total, start, GROUP_IMG, 0) + pool_round
        total = lax.dynamic_update_slice_in_dim(total, block, start, 0)
        total = total.at[slot_images].add(slot_round)
        return (total, None)
    total, _ = lax.scan(device_step, jnp.zeros((images, L, D), jnp.float32), (jnp.arange(devices, dtype=jnp.int32), grads_all, firsts_all, seconds_all))
    incoming_gradient = total.reshape(images * L, D)
    feature_grad = inv_rms * (incoming_gradient - normed * lax.optimization_barrier(jnp.mean(incoming_gradient * normed, axis=-1, keepdims=True)))
    token_grad = jnp.dot(feature_grad.astype(jnp.bfloat16), proj_weight.T, preferred_element_type=jnp.float32)
    return token_grad.astype(jnp.bfloat16).reshape(images, L, D)
```

```python
import functools

import jax
import jax.numpy as jnp
from jax import lax
from jax.experimental import pallas as pl
from jax.experimental.pallas import tpu as pltpu
from jax.sharding import PartitionSpec as P

EPSILON = 1e-05
SOFTMAX_COOLING = 0.1
MESH = pl.DeviceIdType.MESH
LANES = 128
VMEM_LIMIT = 40 * 1024 * 1024
GRID = (4, 8, 2)


def place_of(offset, ring):
    offset %= ring
    return 0 if offset == 0 else 2 * offset - 1 if 2 * offset <= ring else 2 * (ring - offset)


class Where:
    def __init__(self, grid, ring_z):
        _, self.ring_y, cores = grid
        self.cores, self.ring_z, self.peers = cores, ring_z, grid[0] * cores
        grp = lax.axis_index("grp")
        self.z = lax.axis_index("sub")
        self.y = lax.rem(lax.div(grp, cores), self.ring_y)
        self.s = lax.div(grp, cores * self.ring_y) * cores + lax.rem(grp, cores)

    def group(self, s, y):
        return (lax.div(s, self.cores) * self.ring_y + y) * self.cores + lax.rem(s, self.cores)

    def along_y(self, step):
        return {"grp": self.group(self.s, lax.rem(self.y + step + self.ring_y, self.ring_y))}

    def z_at(self, step):
        return lax.rem(self.z + step + self.ring_z, self.ring_z)

    def along_z(self, step):
        return {"sub": self.z_at(step)}

    def s_at(self, turn):
        return lax.rem(self.s + turn, self.peers)

    def across(self, turn):
        return {"grp": self.group(self.s_at(turn), self.y)}

    def greet(self):
        barrier = pltpu.get_barrier_semaphore()
        others = [self.along_y(1), self.along_y(-1), self.along_z(1), self.along_z(-1)]
        others += [self.across(turn) for turn in range(1, self.peers)]
        for other in others:
            pl.semaphore_signal(barrier, inc=1, device_id=other, device_id_type=MESH)
        return lambda: pl.semaphore_wait(barrier, len(others))


def send(src, dst, send_sem, recv_sem, device):
    copy = pltpu.make_async_remote_copy(
        src_ref=src,
        dst_ref=dst,
        send_sem=send_sem,
        recv_sem=recv_sem,
        device_id=device,
        device_id_type=MESH,
    )
    copy.start()
    return copy


def batches(ring):
    half = ring // 2
    return [(0, 1)] + [(2 * d - 1, 2) for d in range(1, half)] + [(ring - 1, 1)]


def rows_at(index, count):
    return pl.ds(pl.multiple_of(index * count, count), count)


def chooser(pick_row, images, length):
    shape = (images * length, pick_row.shape[1])
    row = lax.broadcasted_iota(jnp.int32, shape, 0)
    column = lax.broadcasted_iota(jnp.int32, shape, 1)
    image = lax.div(row, length).astype(jnp.float32)
    same = lax.rem(row, length) == lax.rem(column, length)
    return jnp.where(same & (image == pick_row), 1.0, 0.0).astype(jnp.bfloat16)


def gather_kernel(
    grid,
    ring_z,
    images,
    length,
    picks,
    tokens,
    weight,
    grads,
    seconds,
    pool,
    received,
    laid,
    places,
    pick_rows,
    feature,
    blocks,
    stage,
    y_send,
    y_recv,
    z_send,
    z_recv,
    x_send,
    x_recv,
):
    here = Where(grid, ring_z)
    ring_y, peers = here.ring_y, here.peers
    rows, width = tokens.shape
    block_rows = blocks.shape[1]
    met = here.greet()

    projected = jnp.dot(tokens[...], weight[...], preferred_element_type=jnp.float32)
    feature[...] = projected
    mean_square = jnp.mean(projected * projected, axis=-1, keepdims=True)
    normed = (projected * lax.rsqrt(mean_square + EPSILON)).astype(jnp.bfloat16)
    blocks[0, :rows] = normed
    pool[here.z] = normed
    tail = (block_rows - rows, peers * length)
    tail_row = lax.broadcasted_iota(jnp.int32, tail, 0)
    tail_peer = lax.div(lax.broadcasted_iota(jnp.int32, tail, 1), length)
    table = jnp.zeros(tail, jnp.int32)
    for y in range(ring_y):
        for s in range(peers):
            slot = (s // here.cores * ring_y + y) * here.cores + s % here.cores
            table = jnp.where((tail_row == y) & (tail_peer == s), picks[slot], table)
    blocks[0, rows:] = table.astype(jnp.float32).astype(jnp.bfloat16)
    met()

    half_y, half_z = ring_y // 2, ring_z // 2
    y_copies, z_copies, x_copies = [], [], []

    def forward_y(step):
        for way, turn in enumerate((1, -1)):
            part = slice(0, block_rows)
            if step == half_y:
                part = slice(0, rows // 2) if way == 0 else slice(rows // 2, block_rows)
            part = pl.ds(part.start, part.stop - part.start)
            y_copies.append(
                send(
                    blocks.at[place_of(-turn * (step - 1), ring_y), part],
                    blocks.at[place_of(-turn * step, ring_y), part],
                    y_send.at[way, step - 1],
                    y_recv.at[way, step - 1],
                    here.along_y(turn),
                )
            )

    def forward_z(step):
        for way, turn in enumerate((1, -1)):
            part = pl.ds(0, rows) if step < half_z else pl.ds(way * (rows // 2), rows // 2)
            owner = here.z_at(-turn * (step - 1))
            z_copies.append(
                send(
                    pool.at[owner, part],
                    pool.at[owner, part],
                    z_send.at[way, step - 1],
                    z_recv.at[way, step - 1],
                    here.along_z(turn),
                )
            )

    own = rows_at(here.s, length)

    def choose(batch, place, count):
        for at in range(place, place + count):
            rows_of_y = blocks[at, rows:].astype(jnp.float32)
            mine = jnp.sum(jnp.where(tail_row == here.y, rows_of_y, 0.0), axis=0, keepdims=True)
            pick_rows[at] = jnp.broadcast_to(mine, pick_rows.shape[1:])
            stage[at] = lax.dot_general(
                chooser(mine, images, length),
                blocks[at, :rows],
                (((0,), (0,)), ((), ())),
                preferred_element_type=jnp.float32,
            ).astype(jnp.bfloat16)
        for turn in range(1, peers):
            x_copies.append(
                send(
                    stage.at[pl.ds(place, count), rows_at(here.s_at(turn), length)],
                    received.at[pl.ds(place, count), own],
                    x_send.at[batch, turn - 1],
                    x_recv.at[batch, turn - 1],
                    here.across(turn),
                )
            )
        for at in range(place, place + count):
            received[at, own] = stage[at, own]

    forward_y(1)
    forward_z(1)
    plan = batches(ring_y)
    choose(0, *plan[0])

    slot = seconds[...]
    offset = lax.rem(lax.rem(lax.div(slot, here.cores), ring_y) - here.y + ring_y, ring_y)
    near = jnp.where(2 * offset <= ring_y, 2 * offset - 1, 2 * (ring_y - offset))
    place = jnp.where(offset == 0, 0, near)
    peer = lax.div(slot, here.cores * ring_y) * here.cores + lax.rem(slot, here.cores)
    places[...] = place * peers + peer

    across = LANES // length
    groups = grads.shape[0] // across
    lane_block = lax.div(lax.broadcasted_iota(jnp.int32, (groups, LANES), 1), length)

    def lay(tile):
        wide = grads[:, tile * LANES : (tile + 1) * LANES].astype(jnp.float32)
        parts = [wide[q * groups : (q + 1) * groups] for q in range(across)]
        for r in range(across):
            total = None
            for q in range(across):
                shift = (q - r) % across * length
                moved = pltpu.roll(parts[q], shift, 1) if shift else parts[q]
                total = moved if total is None else jnp.where(lane_block == q, moved, total)
            i = tile * across + r
            laid[i * groups : (i + 1) * groups] = total

    tiles = grads.shape[1] // LANES
    todo = list(range(tiles))
    for step in range(1, max(half_y, half_z) + 1):
        if todo:
            lay(todo.pop(0))
        if step <= half_y:
            for copy in y_copies[2 * step - 2 : 2 * step]:
                copy.wait_recv()
            if step < half_y:
                forward_y(step + 1)
        if step <= half_z:
            for copy in z_copies[2 * step - 2 : 2 * step]:
                copy.wait_recv()
            if step < half_z:
                forward_z(step + 1)
        if step <= half_y:
            choose(step, *plan[step])
    for tile in todo:
        lay(tile)
    for copy in x_copies:
        copy.wait_recv()
    for copy in y_copies + z_copies + x_copies:
        copy.wait_send()


def pair_kernel(
    length,
    first_ref,
    place_ref,
    pool,
    received,
    laid,
    pool_part,
    slot_part,
    pool_total,
    slot_total,
):
    pairs = first_ref.shape[1]
    across = LANES // length
    groups = pairs // across
    width = pool.shape[1]
    scale = 1.0 / (width * SOFTMAX_COOLING)
    together = 4

    pool_total[...] = jnp.zeros_like(pool_total)
    slot_total[...] = jnp.zeros_like(slot_total)
    side = (LANES, LANES)
    row_block = lax.div(lax.broadcasted_iota(jnp.int32, side, 0), length)
    lane_block = lax.div(lax.broadcasted_iota(jnp.int32, side, 1), length)
    diagonal = row_block == lane_block
    ones = jnp.where(diagonal, 1.0, 0.0).astype(jnp.bfloat16)
    ones = jnp.concatenate([ones, ones], axis=0)
    narrow = lax.div(lax.broadcasted_iota(jnp.int32, (length, LANES), 1), length)

    def block_sums(values):
        high = values.astype(jnp.bfloat16)
        low = (values - high.astype(jnp.float32)).astype(jnp.bfloat16)
        return jnp.dot(
            jnp.concatenate([high, low], axis=1), ones, preferred_element_type=jnp.float32
        )

    def step(chunk, carry):
        firsts, seconds, f_at, s_at, scores, incoming = [], [], [], [], [], []
        for n in range(together):
            g = chunk * together + n
            f_at.append([rows_at(first_ref[0, q * groups + g], length) for q in range(across)])
            s_at.append([rows_at(place_ref[0, q * groups + g], length) for q in range(across)])
            firsts.append(jnp.concatenate([pool[at] for at in f_at[n]], axis=0))
            seconds.append(jnp.concatenate([received[at] for at in s_at[n]], axis=0))
            full = lax.dot_general(
                firsts[n],
                seconds[n],
                (((1,), (1,)), ((), ())),
                preferred_element_type=jnp.float32,
            )
            packed = full[:length]
            for q in range(1, across):
                packed = jnp.where(narrow == q, full[q * length : (q + 1) * length], packed)
            scores.append(packed)
            incoming.append(laid[pl.ds(g, length, stride=groups), :])
        shape = (together, length, LANES)
        expo = jnp.exp(jnp.concatenate(scores, axis=0) * scale)
        gradient = jnp.concatenate(incoming, axis=0)
        rows = expo / block_sums(expo)
        expo = expo.reshape(shape)
        cols = (expo / jnp.sum(expo, axis=1, keepdims=True)).reshape(rows.shape)
        both = gradient * rows * cols
        over_second = block_sums(both)
        over_first = jnp.sum(both.reshape(shape), axis=1, keepdims=True)
        part = (cols.reshape(shape) * over_first).reshape(rows.shape)
        d_scaled = ((2.0 * both - rows * over_second - part) * scale).astype(jnp.bfloat16)
        for n in range(together):
            mine = d_scaled[n * length : (n + 1) * length]
            wide = jnp.concatenate([mine] * across, axis=0)
            wide = jnp.where(diagonal, wide, jnp.zeros_like(wide))
            grad_first = jnp.dot(wide, seconds[n], preferred_element_type=jnp.float32)
            grad_second = lax.dot_general(
                wide, firsts[n], (((0,), (0,)), ((), ())), preferred_element_type=jnp.float32
            )
            for q in range(across):
                part = slice(q * length, (q + 1) * length)
                pool_total[f_at[n][q]] += grad_first[part]
                slot_total[s_at[n][q]] += grad_second[part]
        return carry

    lax.fori_loop(0, groups // together, step, 0)
    pool_part[...] = pool_total[...].astype(jnp.bfloat16)
    slot_part[...] = slot_total[...].astype(jnp.bfloat16)


def return_kernel(
    grid,
    ring_z,
    images,
    length,
    slots,
    pool,
    pick_rows,
    feature,
    feature_grad,
    arrived,
    choosers,
    y_in,
    y_out,
    z_in,
    z_out,
    y_send,
    y_recv,
    z_send,
    z_recv,
    x_send,
    x_recv,
):
    here = Where(grid, ring_z)
    ring_y, peers = here.ring_y, here.peers
    rows, width = feature.shape
    half_y, half_z = ring_y // 2, ring_z // 2
    met = here.greet()
    own = rows_at(here.s, length)
    plan = batches(ring_y)
    met()

    y_copies, z_copies, x_copies = [], [], {}

    def ring_z_send(step, source_of):
        for way, turn in enumerate((1, -1)):
            part = pl.ds(way * (rows // 2), rows // 2) if step == 1 else pl.ds(0, rows)
            z_copies.append(
                send(
                    source_of(way, turn).at[part],
                    z_in.at[way, step - 1, part],
                    z_send.at[way, step - 1],
                    z_recv.at[way, step - 1],
                    here.along_z(turn),
                )
            )

    def ring_y_send(step):
        for way, turn in enumerate((1, -1)):
            part = pl.ds(way * (rows // 2), rows // 2) if step == 1 else pl.ds(0, rows)
            y_copies.append(
                send(
                    y_out.at[way, step - 1, part],
                    y_in.at[way, step - 1, part],
                    y_send.at[way, step - 1],
                    y_recv.at[way, step - 1],
                    here.along_y(turn),
                )
            )

    ring_z_send(1, lambda way, turn: pool.at[here.z_at(turn * half_z)])
    for distance in range(half_y, -1, -1):
        place, count = plan[distance]
        x_copies[distance] = [
            send(
                slots.at[pl.ds(place, count), rows_at(here.s_at(turn), length)],
                arrived.at[pl.ds(place, count), own],
                x_send.at[distance, turn - 1],
                x_recv.at[distance, turn - 1],
                here.across(turn),
            )
            for turn in range(1, peers)
        ]
    for at in range(ring_y):
        arrived[at, own] = slots[at, own]
        choosers[at] = chooser(pick_rows[at, :1], images, length)

    def summed(place):
        return jnp.dot(choosers[place], arrived[place], preferred_element_type=jnp.float32)

    def wait_x(distance):
        for copy in x_copies[distance]:
            copy.wait_recv()

    def joined(total, ins, way, step):
        if step > 1:
            return total + ins[way, step - 1].astype(jnp.float32)
        low = way * (rows // 2)
        added = total[low : low + rows // 2] + ins[way, 0, low : low + rows // 2].astype(jnp.float32)
        rest = total[rows // 2 :] if way == 0 else total[: rows // 2]
        return jnp.concatenate([added, rest] if way == 0 else [rest, added], axis=0)

    for step in range(1, max(half_y, half_z) + 1):
        if 1 < step <= half_z:
            for copy in z_copies[2 * step - 4 : 2 * step - 2]:
                copy.wait_recv()
            for way, turn in enumerate((1, -1)):
                mine = pool[here.z_at(turn * (half_z - step + 1))].astype(jnp.float32)
                z_out[way, step - 1] = joined(mine, z_in, way, step - 1).astype(jnp.bfloat16)
            ring_z_send(step, lambda way, turn: z_out.at[way, step - 1])
        if step <= half_y:
            distance = half_y - step + 1
            wait_x(distance)
            if step == 1:
                total = summed(ring_y - 1)
                for way in range(2):
                    y_out[way, 0] = total.astype(jnp.bfloat16)
            else:
                totals = [summed(place_of(turn * distance, ring_y)) for turn in (1, -1)]
                for copy in y_copies[2 * step - 4 : 2 * step - 2]:
                    copy.wait_recv()
                for way in range(2):
                    y_out[way, step - 1] = joined(totals[way], y_in, way, step - 1).astype(
                        jnp.bfloat16
                    )
            ring_y_send(step)
    wait_x(0)
    gradient = summed(0) + pool[here.z].astype(jnp.float32)
    projected = feature[...]
    mean_square = jnp.mean(projected * projected, axis=-1, keepdims=True)
    inv_rms = lax.rsqrt(mean_square + EPSILON)
    normed = projected * inv_rms
    for copy in y_copies[2 * half_y - 2 :] + z_copies[2 * half_z - 2 :]:
        copy.wait_recv()
    for way in range(2):
        gradient = joined(gradient, y_in, way, half_y)
        gradient = joined(gradient, z_in, way, half_z)
    mean = jnp.mean(gradient * normed, axis=-1, keepdims=True)
    feature_grad[...] = (inv_rms * (gradient - normed * mean)).astype(jnp.bfloat16)
    for copy in y_copies + z_copies + sum(x_copies.values(), []):
        copy.wait_send()


def in_vmem(count):
    return [pl.BlockSpec(memory_space=pltpu.VMEM)] * count


def in_smem(count):
    return [pl.BlockSpec(memory_space=pltpu.SMEM)] * count


def ring_semaphores(half_y, half_z, peers):
    dma = pltpu.SemaphoreType.DMA
    pairs = [(2, half_y), (2, half_z), (half_y + 1, peers - 1)]
    return [dma(shape) for shape in pairs for _ in range(2)]


def local(grid, ring_z, tokens, proj_weight, match_grad, edge_first, pair_second_image, send_pick):
    images, length, width = tokens.shape
    rows = images * length
    pairs = edge_first.shape[0]
    ring_y, peers = grid[1], grid[0] * grid[2]
    half_y, half_z = ring_y // 2, ring_z // 2
    bf16, f32 = jnp.bfloat16, jnp.float32
    shape = jax.ShapeDtypeStruct

    pool, received, laid, places, pick_rows, feature = pl.pallas_call(
        functools.partial(gather_kernel, grid, ring_z, images, length),
        out_shape=(
            shape((ring_z, rows, width), bf16),
            shape((ring_y, peers * length, width), bf16),
            shape((pairs * length * length // LANES, LANES), f32),
            shape((1, pairs), jnp.int32),
            shape((ring_y, 8, peers * length), f32),
            shape((rows, width), f32),
        ),
        in_specs=in_smem(1) + in_vmem(4),
        out_specs=tuple(in_vmem(6)),
        scratch_shapes=[
            pltpu.VMEM((ring_y, rows + 16, width), bf16),
            pltpu.VMEM((ring_y, peers * length, width), bf16),
            *ring_semaphores(half_y, half_z, peers),
        ],
        compiler_params=pltpu.CompilerParams(
            collective_id=0, has_side_effects=True, vmem_limit_bytes=VMEM_LIMIT
        ),
        name="gather_images",
    )(
        send_pick,
        tokens.reshape(rows, width),
        proj_weight,
        match_grad,
        pair_second_image.reshape(1, pairs),
    )

    pool_part, slot_part = pl.pallas_call(
        functools.partial(pair_kernel, length),
        out_shape=(
            shape((ring_z * rows, width), bf16),
            shape((ring_y * peers * length, width), bf16),
        ),
        in_specs=in_smem(2) + in_vmem(3),
        out_specs=tuple(in_vmem(2)),
        scratch_shapes=[
            pltpu.VMEM((ring_z * rows, width), f32),
            pltpu.VMEM((ring_y * peers * length, width), f32),
        ],
        compiler_params=pltpu.CompilerParams(vmem_limit_bytes=VMEM_LIMIT),
        name="pair_gradients",
    )(
        edge_first.reshape(1, pairs),
        places,
        pool.reshape(ring_z * rows, width),
        received.reshape(ring_y * peers * length, width),
        laid,
    )

    feature_grad = pl.pallas_call(
        functools.partial(return_kernel, grid, ring_z, images, length),
        out_shape=shape((rows, width), bf16),
        in_specs=in_vmem(4),
        out_specs=pl.BlockSpec(memory_space=pltpu.VMEM),
        scratch_shapes=[
            pltpu.VMEM((ring_y, peers * length, width), bf16),
            pltpu.VMEM((ring_y, rows, peers * length), bf16),
            pltpu.VMEM((2, half_y, rows, width), bf16),
            pltpu.VMEM((2, half_y, rows, width), bf16),
            pltpu.VMEM((2, half_z, rows, width), bf16),
            pltpu.VMEM((2, half_z, rows, width), bf16),
            *ring_semaphores(half_y, half_z, peers),
        ],
        compiler_params=pltpu.CompilerParams(
            collective_id=1, has_side_effects=True, vmem_limit_bytes=VMEM_LIMIT
        ),
        name="return_gradients",
    )(
        slot_part.reshape(ring_y, peers * length, width),
        pool_part.reshape(ring_z, rows, width),
        pick_rows,
        feature,
    )
    token_grad = lax.dot_general(
        feature_grad, proj_weight, (((1,), (1,)), ((), ())), preferred_element_type=f32
    )
    return token_grad.astype(bf16).reshape(images, length, width)


def solution(mesh, grid=GRID):
    placed = (
        P(("grp", "sub"), None, None),
        P(),
        P(("grp", "sub"), None),
        P(("grp", "sub")),
        P(("grp", "sub")),
        P(("grp", "sub")),
    )
    return jax.shard_map(
        functools.partial(local, grid, mesh.shape["sub"]),
        mesh=mesh,
        in_specs=placed,
        out_specs=P(("grp", "sub"), None, None),
        check_vma=False,
    )
```

```python
import functools

import jax
import jax.numpy as jnp
from jax import lax
from jax.experimental import pallas as pl
from jax.experimental.pallas import tpu as pltpu
from jax.sharding import PartitionSpec as P

EPSILON = 1e-05
SOFTMAX_COOLING = 0.1
MESH = pl.DeviceIdType.MESH
LANES = 128
VMEM_LIMIT = 40 * 1024 * 1024
GRID = (4, 8, 2)
STEPS_Y = {1: 0, 2: 0, 3: 2, 4: 2}
STEPS_Z = {2: 0, 1: 0, 4: 2, 3: 2, 6: 4, 5: 4}


def place_of(offset, ring):
    offset %= ring
    return 0 if offset == 0 else 2 * offset - 1 if 2 * offset <= ring else 2 * (ring - offset)


class Where:
    def __init__(self, grid, ring_z):
        _, self.ring_y, cores = grid
        self.cores, self.ring_z, self.peers = cores, ring_z, grid[0] * cores
        grp = lax.axis_index("grp")
        self.z = lax.axis_index("sub")
        self.y = lax.rem(lax.div(grp, cores), self.ring_y)
        self.s = lax.div(grp, cores * self.ring_y) * cores + lax.rem(grp, cores)

    def group(self, s, y):
        return (lax.div(s, self.cores) * self.ring_y + y) * self.cores + lax.rem(s, self.cores)

    def along_y(self, step):
        return {"grp": self.group(self.s, lax.rem(self.y + step + self.ring_y, self.ring_y))}

    def z_at(self, step):
        return lax.rem(self.z + step + self.ring_z, self.ring_z)

    def along_z(self, step):
        return {"sub": self.z_at(step)}

    def s_at(self, turn):
        return lax.rem(self.s + turn, self.peers)

    def across(self, turn):
        return {"grp": self.group(self.s_at(turn), self.y)}

    def greet(self, steps_y, steps_z):
        barrier = pltpu.get_barrier_semaphore()
        others = []
        for hop in sorted({distance - before for distance, before in steps_y.items()}):
            others += [self.along_y(hop), self.along_y(-hop)]
        for hop in sorted({distance - before for distance, before in steps_z.items()}):
            others += [self.along_z(hop), self.along_z(-hop)]
        others += [self.across(turn) for turn in range(1, self.peers)]
        for other in others:
            pl.semaphore_signal(barrier, inc=1, device_id=other, device_id_type=MESH)
        return lambda: pl.semaphore_wait(barrier, len(others))


def send(src, dst, send_sem, recv_sem, device):
    copy = pltpu.make_async_remote_copy(
        src_ref=src,
        dst_ref=dst,
        send_sem=send_sem,
        recv_sem=recv_sem,
        device_id=device,
        device_id_type=MESH,
    )
    copy.start()
    return copy


def batches(ring):
    half = ring // 2
    return [(0, 1)] + [(2 * d - 1, 2) for d in range(1, half)] + [(ring - 1, 1)]


def rows_at(index, count):
    return pl.ds(pl.multiple_of(index * count, count), count)


def chooser(pick_row, images, length):
    shape = (images * length, pick_row.shape[1])
    row = lax.broadcasted_iota(jnp.int32, shape, 0)
    column = lax.broadcasted_iota(jnp.int32, shape, 1)
    image = lax.div(row, length).astype(jnp.float32)
    same = lax.rem(row, length) == lax.rem(column, length)
    return jnp.where(same & (image == pick_row), 1.0, 0.0).astype(jnp.bfloat16)


def gather_kernel(
    grid,
    ring_z,
    steps_y,
    steps_z,
    images,
    length,
    picks_arg,
    tokens_arg,
    weight_arg,
    grads_arg,
    firsts_arg,
    seconds_arg,
    pool,
    received,
    laid,
    firsts,
    places,
    pick_rows,
    feature,
    pool_zero,
    slot_zero,
    picks,
    tokens,
    weight,
    grads,
    seconds,
    blocks,
    stage,
    fetch_sem,
    y_send,
    y_recv,
    z_send,
    z_recv,
    x_send,
    x_recv,
):
    here = Where(grid, ring_z)
    ring_y, peers = here.ring_y, here.peers
    rows, width = tokens.shape
    block_rows = blocks.shape[1]
    fetches = [
        pltpu.make_async_copy(src, dst, fetch_sem.at[n])
        for n, (src, dst) in enumerate(
            (
                (tokens_arg, tokens),
                (weight_arg, weight),
                (picks_arg, picks),
                (seconds_arg, seconds),
                (firsts_arg, firsts),
                (grads_arg, grads),
            )
        )
    ]
    for fetch in fetches:
        fetch.start()
    met = here.greet(steps_y, steps_z)

    for fetch in fetches[:3]:
        fetch.wait()
    projected = jnp.dot(tokens[...], weight[...], preferred_element_type=jnp.float32)
    feature[...] = projected
    mean_square = jnp.mean(projected * projected, axis=-1, keepdims=True)
    normed = (projected * lax.rsqrt(mean_square + EPSILON)).astype(jnp.bfloat16)
    blocks[0, :rows] = normed
    pool[here.z] = normed
    tail = (block_rows - rows, peers * length)
    tail_row = lax.broadcasted_iota(jnp.int32, tail, 0)
    tail_peer = lax.div(lax.broadcasted_iota(jnp.int32, tail, 1), length)
    table = jnp.zeros(tail, jnp.int32)
    for y in range(ring_y):
        for s in range(peers):
            slot = (s // here.cores * ring_y + y) * here.cores + s % here.cores
            table = jnp.where((tail_row == y) & (tail_peer == s), picks[slot], table)
    blocks[0, rows:] = table.astype(jnp.float32).astype(jnp.bfloat16)
    met()

    half_y, half_z = ring_y // 2, ring_z // 2
    y_copies, z_copies, x_copies = {}, {}, []

    def forward_y(source):
        for distance, before in steps_y.items():
            if before != source:
                continue
            for way, turn in enumerate((1, -1)):
                part = pl.ds(0, block_rows)
                if distance == half_y:
                    part = pl.ds(0, rows // 2) if way == 0 else pl.ds(rows // 2, block_rows - rows // 2)
                y_copies[distance, way] = send(
                    blocks.at[place_of(-turn * before, ring_y), part],
                    blocks.at[place_of(-turn * distance, ring_y), part],
                    y_send.at[way, distance - 1],
                    y_recv.at[way, distance - 1],
                    here.along_y(turn * (distance - before)),
                )

    def forward_z(source):
        for distance, before in steps_z.items():
            if before != source:
                continue
            for way, turn in enumerate((1, -1)):
                part = pl.ds(way * (rows // 2), rows // 2) if distance == half_z else pl.ds(0, rows)
                owner = here.z_at(-turn * before)
                z_copies[distance, way] = send(
                    pool.at[owner, part],
                    pool.at[owner, part],
                    z_send.at[way, distance - 1],
                    z_recv.at[way, distance - 1],
                    here.along_z(turn * (distance - before)),
                )

    own = rows_at(here.s, length)

    def choose(batch, place, count):
        for at in range(place, place + count):
            rows_of_y = blocks[at, rows:].astype(jnp.float32)
            mine = jnp.sum(jnp.where(tail_row == here.y, rows_of_y, 0.0), axis=0, keepdims=True)
            pick_rows[at] = jnp.broadcast_to(mine, pick_rows.shape[1:])
            stage[at] = lax.dot_general(
                chooser(mine, images, length),
                blocks[at, :rows],
                (((0,), (0,)), ((), ())),
                preferred_element_type=jnp.float32,
            ).astype(jnp.bfloat16)
        for turn in range(1, peers):
            x_copies.append(
                send(
                    stage.at[pl.ds(place, count), rows_at(here.s_at(turn), length)],
                    received.at[pl.ds(place, count), own],
                    x_send.at[batch, turn - 1],
                    x_recv.at[batch, turn - 1],
                    here.across(turn),
                )
            )
        for at in range(place, place + count):
            received[at, own] = stage[at, own]

    forward_y(0)
    forward_z(0)
    plan = batches(ring_y)
    choose(0, *plan[0])
    for fetch in fetches[3:]:
        fetch.wait()

    slot = seconds[...]
    offset = lax.rem(lax.rem(lax.div(slot, here.cores), ring_y) - here.y + ring_y, ring_y)
    near = jnp.where(2 * offset <= ring_y, 2 * offset - 1, 2 * (ring_y - offset))
    place = jnp.where(offset == 0, 0, near)
    peer = lax.div(slot, here.cores * ring_y) * here.cores + lax.rem(slot, here.cores)
    places[...] = place * peers + peer

    across = LANES // length
    groups = grads.shape[0] // across
    lane_block = lax.div(lax.broadcasted_iota(jnp.int32, (groups, LANES), 1), length)

    def lay(tile):
        wide = grads[:, tile * LANES : (tile + 1) * LANES].astype(jnp.float32)
        parts = [wide[q * groups : (q + 1) * groups] for q in range(across)]
        for r in range(across):
            total = None
            for q in range(across):
                shift = (q - r) % across * length
                moved = pltpu.roll(parts[q], shift, 1) if shift else parts[q]
                total = moved if total is None else jnp.where(lane_block == q, moved, total)
            i = tile * across + r
            laid[i * groups : (i + 1) * groups] = total

    tiles = grads.shape[1] // LANES
    todo = list(range(tiles))
    for distance in range(1, max(half_y, half_z) + 1):
        if todo:
            lay(todo.pop(0))
        if distance <= half_y:
            for way in range(2):
                y_copies[distance, way].wait_recv()
            forward_y(distance)
        if distance <= half_z:
            for way in range(2):
                z_copies[distance, way].wait_recv()
            forward_z(distance)
        if distance <= half_y:
            choose(distance, *plan[distance])
    for tile in todo:
        lay(tile)
    pool_zero[...] = jnp.zeros_like(pool_zero)
    slot_zero[...] = jnp.zeros_like(slot_zero)
    for copy in x_copies:
        copy.wait_recv()
    for copy in [*y_copies.values(), *z_copies.values(), *x_copies]:
        copy.wait_send()


def pair_kernel(
    length,
    first_ref,
    place_ref,
    pool,
    received,
    laid,
    pool_zero,
    slot_zero,
    pool_total,
    slot_total,
):
    pairs = first_ref.shape[1]
    across = LANES // length
    groups = pairs // across
    width = pool.shape[1]
    scale = 1.0 / (width * SOFTMAX_COOLING)
    together = 4

    del pool_zero, slot_zero
    side = (LANES, LANES)
    row_block = lax.div(lax.broadcasted_iota(jnp.int32, side, 0), length)
    lane_block = lax.div(lax.broadcasted_iota(jnp.int32, side, 1), length)
    diagonal = row_block == lane_block
    ones = jnp.where(diagonal, 1.0, 0.0).astype(jnp.bfloat16)
    ones = jnp.concatenate([ones, ones], axis=0)
    narrow = lax.div(lax.broadcasted_iota(jnp.int32, (length, LANES), 1), length)

    def block_sums(values):
        high = values.astype(jnp.bfloat16)
        low = (values - high.astype(jnp.float32)).astype(jnp.bfloat16)
        return jnp.dot(
            jnp.concatenate([high, low], axis=1), ones, preferred_element_type=jnp.float32
        )

    def step(chunk, carry):
        firsts, seconds, f_at, s_at, scores, incoming = [], [], [], [], [], []
        for n in range(together):
            g = chunk * together + n
            f_at.append([rows_at(first_ref[0, q * groups + g], length) for q in range(across)])
            s_at.append([rows_at(place_ref[0, q * groups + g], length) for q in range(across)])
            firsts.append(jnp.concatenate([pool[at] for at in f_at[n]], axis=0))
            seconds.append(jnp.concatenate([received[at] for at in s_at[n]], axis=0))
            full = lax.dot_general(
                firsts[n],
                seconds[n],
                (((1,), (1,)), ((), ())),
                preferred_element_type=jnp.float32,
            )
            packed = full[:length]
            for q in range(1, across):
                packed = jnp.where(narrow == q, full[q * length : (q + 1) * length], packed)
            scores.append(packed)
            incoming.append(laid[pl.ds(g, length, stride=groups), :])
        shape = (together, length, LANES)
        expo = jnp.exp(jnp.concatenate(scores, axis=0) * scale)
        gradient = jnp.concatenate(incoming, axis=0)
        rows = expo / block_sums(expo)
        expo = expo.reshape(shape)
        cols = (expo / jnp.sum(expo, axis=1, keepdims=True)).reshape(rows.shape)
        both = gradient * rows * cols
        over_second = block_sums(both)
        over_first = jnp.sum(both.reshape(shape), axis=1, keepdims=True)
        part = (cols.reshape(shape) * over_first).reshape(rows.shape)
        d_scaled = ((2.0 * both - rows * over_second - part) * scale).astype(jnp.bfloat16)
        for n in range(together):
            mine = d_scaled[n * length : (n + 1) * length]
            wide = jnp.concatenate([mine] * across, axis=0)
            wide = jnp.where(diagonal, wide, jnp.zeros_like(wide))
            grad_first = jnp.dot(wide, seconds[n], preferred_element_type=jnp.float32)
            grad_second = lax.dot_general(
                wide, firsts[n], (((0,), (0,)), ((), ())), preferred_element_type=jnp.float32
            )
            for q in range(across):
                part = slice(q * length, (q + 1) * length)
                pool_total[f_at[n][q]] += grad_first[part]
                slot_total[s_at[n][q]] += grad_second[part]
        return carry

    lax.fori_loop(0, groups // together, step, 0)


def return_kernel(
    grid,
    ring_z,
    steps_y,
    steps_z,
    images,
    length,
    slot_total,
    pool_total,
    pick_rows,
    feature,
    feature_grad,
    slots,
    pool,
    arrived,
    choosers,
    y_in,
    y_out,
    z_in,
    z_out,
    y_send,
    y_recv,
    z_send,
    z_recv,
    x_send,
    x_recv,
):
    here = Where(grid, ring_z)
    ring_y, peers = here.ring_y, here.peers
    rows, width = feature.shape
    half_y, half_z = ring_y // 2, ring_z // 2
    met = here.greet(steps_y, steps_z)
    own = rows_at(here.s, length)
    plan = batches(ring_y)
    slots[...] = slot_total[...].astype(jnp.bfloat16)
    pool[...] = pool_total[...].astype(jnp.bfloat16)
    met()

    y_copies, z_copies, x_copies = {}, {}, {}

    def part_of(distance, way, half):
        return pl.ds(way * (rows // 2), rows // 2) if distance == half else pl.ds(0, rows)

    def send_z(distance):
        hop = distance - steps_z[distance]
        for way, turn in enumerate((1, -1)):
            part = part_of(distance, way, half_z)
            if distance in steps_z.values():
                source = z_out.at[way, distance - 1, part]
            else:
                source = pool.at[here.z_at(turn * distance), part]
            z_copies[distance, way] = send(
                source,
                z_in.at[way, distance - 1, part],
                z_send.at[way, distance - 1],
                z_recv.at[way, distance - 1],
                here.along_z(turn * hop),
            )

    def send_y(distance):
        hop = distance - steps_y[distance]
        for way, turn in enumerate((1, -1)):
            part = part_of(distance, way, half_y)
            y_copies[distance, way] = send(
                y_out.at[way, distance - 1, part],
                y_in.at[way, distance - 1, part],
                y_send.at[way, distance - 1],
                y_recv.at[way, distance - 1],
                here.along_y(turn * hop),
            )

    for distance in range(half_z, 0, -1):
        if distance not in steps_z.values():
            send_z(distance)
    for distance in range(half_y, -1, -1):
        place, count = plan[distance]
        x_copies[distance] = [
            send(
                slots.at[pl.ds(place, count), rows_at(here.s_at(turn), length)],
                arrived.at[pl.ds(place, count), own],
                x_send.at[distance, turn - 1],
                x_recv.at[distance, turn - 1],
                here.across(turn),
            )
            for turn in range(1, peers)
        ]
    for at in range(ring_y):
        arrived[at, own] = slots[at, own]
        choosers[at] = chooser(pick_rows[at, :1], images, length)

    def summed(place):
        return jnp.dot(choosers[place], arrived[place], preferred_element_type=jnp.float32)

    def wait_x(distance):
        for copy in x_copies[distance]:
            copy.wait_recv()

    def joined(total, ins, way, distance, half):
        if distance < half:
            return total + ins[way, distance - 1].astype(jnp.float32)
        low = way * (rows // 2)
        added = ins[way, distance - 1, low : low + rows // 2].astype(jnp.float32)
        added = added + total[low : low + rows // 2]
        rest = total[rows // 2 :] if way == 0 else total[: rows // 2]
        return jnp.concatenate([added, rest] if way == 0 else [rest, added], axis=0)

    def collect(total, way, distance, steps, copies, ins, half):
        for farther in sorted(steps, reverse=True):
            if steps[farther] == distance:
                copies[farther, way].wait_recv()
                total = joined(total, ins, way, farther, half)
        return total

    along_z = (steps_z, z_copies, z_in, half_z)
    along_y = (steps_y, y_copies, y_in, half_y)
    for distance in range(max(half_y, half_z), 0, -1):
        if distance <= half_y:
            wait_x(distance)
            for way, turn in enumerate((1, -1)):
                if distance < half_y or way == 0:
                    mine = summed(place_of(turn * distance, ring_y))
                total = collect(mine, way, distance, *along_y)
                y_out[way, distance - 1] = total.astype(jnp.bfloat16)
            send_y(distance)
        if distance <= half_z and distance in steps_z.values():
            for way, turn in enumerate((1, -1)):
                mine = pool[here.z_at(turn * distance)].astype(jnp.float32)
                total = collect(mine, way, distance, *along_z)
                z_out[way, distance - 1] = total.astype(jnp.bfloat16)
            send_z(distance)
    wait_x(0)
    gradient = summed(0) + pool[here.z].astype(jnp.float32)
    projected = feature[...]
    mean_square = jnp.mean(projected * projected, axis=-1, keepdims=True)
    inv_rms = lax.rsqrt(mean_square + EPSILON)
    normed = projected * inv_rms
    for way in range(2):
        gradient = collect(gradient, way, 0, *along_z)
        gradient = collect(gradient, way, 0, *along_y)
    mean = jnp.mean(gradient * normed, axis=-1, keepdims=True)
    feature_grad[...] = (inv_rms * (gradient - normed * mean)).astype(jnp.bfloat16)
    for copy in [*y_copies.values(), *z_copies.values(), *sum(x_copies.values(), [])]:
        copy.wait_send()


def in_vmem(count):
    return [pl.BlockSpec(memory_space=pltpu.VMEM)] * count


def in_smem(count):
    return [pl.BlockSpec(memory_space=pltpu.SMEM)] * count


def ring_semaphores(half_y, half_z, peers):
    dma = pltpu.SemaphoreType.DMA
    pairs = [(2, half_y), (2, half_z), (half_y + 1, peers - 1)]
    return [dma(shape) for shape in pairs for _ in range(2)]


def local(
    grid,
    ring_z,
    steps_y,
    steps_z,
    tokens,
    proj_weight,
    match_grad,
    edge_first,
    pair_second_image,
    send_pick,
):
    images, length, width = tokens.shape
    rows = images * length
    pairs = edge_first.shape[0]
    ring_y, peers = grid[1], grid[0] * grid[2]
    half_y, half_z = ring_y // 2, ring_z // 2
    layout = (grid, ring_z, steps_y, steps_z, images, length)
    bf16, f32 = jnp.bfloat16, jnp.float32
    shape = jax.ShapeDtypeStruct
    pool_rows, slot_rows = ring_z * rows, ring_y * peers * length

    pool, received, laid, firsts, places, pick_rows, feature, pool_zero, slot_zero = pl.pallas_call(
        functools.partial(gather_kernel, *layout),
        out_shape=(
            shape((ring_z, rows, width), bf16),
            shape((ring_y, peers * length, width), bf16),
            shape((pairs * length * length // LANES, LANES), f32),
            shape((1, pairs), jnp.int32),
            shape((1, pairs), jnp.int32),
            shape((ring_y, 8, peers * length), f32),
            shape((rows, width), f32),
            shape((pool_rows, width), f32),
            shape((slot_rows, width), f32),
        ),
        in_specs=[pl.BlockSpec(memory_space=pltpu.HBM)] * 6,
        out_specs=tuple(in_vmem(9)),
        scratch_shapes=[
            pltpu.SMEM((send_pick.shape[0],), jnp.int32),
            pltpu.VMEM((rows, width), bf16),
            pltpu.VMEM(proj_weight.shape, bf16),
            pltpu.VMEM(match_grad.shape, bf16),
            pltpu.VMEM((1, pairs), jnp.int32),
            pltpu.VMEM((ring_y, rows + 16, width), bf16),
            pltpu.VMEM((ring_y, peers * length, width), bf16),
            pltpu.SemaphoreType.DMA((6,)),
            *ring_semaphores(half_y, half_z, peers),
        ],
        compiler_params=pltpu.CompilerParams(
            collective_id=0, has_side_effects=True, vmem_limit_bytes=VMEM_LIMIT
        ),
        name="gather_images",
    )(
        *(
            pltpu.with_memory_space_constraint(argument, pltpu.HBM)
            for argument in (
                send_pick,
                tokens.reshape(rows, width),
                proj_weight,
                match_grad,
                edge_first.reshape(1, pairs),
                pair_second_image.reshape(1, pairs),
            )
        )
    )

    pool_total, slot_total = pl.pallas_call(
        functools.partial(pair_kernel, length),
        out_shape=(shape((pool_rows, width), f32), shape((slot_rows, width), f32)),
        in_specs=in_smem(2) + in_vmem(5),
        out_specs=tuple(in_vmem(2)),
        input_output_aliases={5: 0, 6: 1},
        compiler_params=pltpu.CompilerParams(vmem_limit_bytes=VMEM_LIMIT),
        name="pair_gradients",
    )(
        firsts,
        places,
        pool.reshape(pool_rows, width),
        received.reshape(slot_rows, width),
        laid,
        pool_zero,
        slot_zero,
    )

    feature_grad = pl.pallas_call(
        functools.partial(return_kernel, *layout),
        out_shape=shape((rows, width), bf16),
        in_specs=in_vmem(4),
        out_specs=pl.BlockSpec(memory_space=pltpu.VMEM),
        scratch_shapes=[
            pltpu.VMEM((ring_y, peers * length, width), bf16),
            pltpu.VMEM((ring_z, rows, width), bf16),
            pltpu.VMEM((ring_y, peers * length, width), bf16),
            pltpu.VMEM((ring_y, rows, peers * length), bf16),
            pltpu.VMEM((2, half_y, rows, width), bf16),
            pltpu.VMEM((2, half_y, rows, width), bf16),
            pltpu.VMEM((2, half_z, rows, width), bf16),
            pltpu.VMEM((2, half_z, rows, width), bf16),
            *ring_semaphores(half_y, half_z, peers),
        ],
        compiler_params=pltpu.CompilerParams(
            collective_id=1, has_side_effects=True, vmem_limit_bytes=VMEM_LIMIT
        ),
        name="return_gradients",
    )(
        slot_total.reshape(ring_y, peers * length, width),
        pool_total.reshape(ring_z, rows, width),
        pick_rows,
        feature,
    )
    token_grad = lax.dot_general(
        feature_grad, proj_weight, (((1,), (1,)), ((), ())), preferred_element_type=f32
    )
    return token_grad.astype(bf16).reshape(images, length, width)


def solution(mesh, grid=GRID, steps_y=STEPS_Y, steps_z=STEPS_Z):
    placed = (
        P(("grp", "sub"), None, None),
        P(),
        P(("grp", "sub"), None),
        P(("grp", "sub")),
        P(("grp", "sub")),
        P(("grp", "sub")),
    )
    return jax.shard_map(
        functools.partial(local, grid, mesh.shape["sub"], steps_y, steps_z),
        mesh=mesh,
        in_specs=placed,
        out_specs=P(("grp", "sub"), None, None),
        check_vma=False,
    )
```

```python
import functools

import jax
import jax.numpy as jnp
from jax import lax
from jax.experimental import pallas as pl
from jax.experimental.pallas import tpu as pltpu
from jax.sharding import PartitionSpec as P

EPSILON = 1e-05
SOFTMAX_COOLING = 0.1
MESH = pl.DeviceIdType.MESH
LANES = 128
VMEM_LIMIT = 40 * 1024 * 1024
GRID = (4, 8, 2)
STEPS_Y = {1: 0, 2: 0, 3: 2, 4: 2}
STEPS_Z = {2: 0, 1: 0, 4: 2, 3: 2, 6: 4, 5: 4}


def place_of(offset, ring):
    offset %= ring
    return 0 if offset == 0 else 2 * offset - 1 if 2 * offset <= ring else 2 * (ring - offset)


class Where:
    def __init__(self, grid, ring_z):
        _, self.ring_y, cores = grid
        self.cores, self.ring_z, self.peers = cores, ring_z, grid[0] * cores
        grp = lax.axis_index("grp")
        self.z = lax.axis_index("sub")
        self.y = lax.rem(lax.div(grp, cores), self.ring_y)
        self.s = lax.div(grp, cores * self.ring_y) * cores + lax.rem(grp, cores)

    def group(self, s, y):
        return (lax.div(s, self.cores) * self.ring_y + y) * self.cores + lax.rem(s, self.cores)

    def along_y(self, step):
        return {"grp": self.group(self.s, lax.rem(self.y + step + self.ring_y, self.ring_y))}

    def z_at(self, step):
        return lax.rem(self.z + step + self.ring_z, self.ring_z)

    def along_z(self, step):
        return {"sub": self.z_at(step)}

    def s_at(self, turn):
        return lax.rem(self.s + turn, self.peers)

    def across(self, turn):
        return {"grp": self.group(self.s_at(turn), self.y)}

    def greet(self, steps_y, steps_z):
        barrier = pltpu.get_barrier_semaphore()
        others = []
        for hop in sorted({distance - before for distance, before in steps_y.items()}):
            others += [self.along_y(hop), self.along_y(-hop)]
        for hop in sorted({distance - before for distance, before in steps_z.items()}):
            others += [self.along_z(hop), self.along_z(-hop)]
        others += [self.across(turn) for turn in range(1, self.peers)]
        for other in others:
            pl.semaphore_signal(barrier, inc=1, device_id=other, device_id_type=MESH)
        return lambda: pl.semaphore_wait(barrier, len(others))


def send(src, dst, send_sem, recv_sem, device):
    copy = pltpu.make_async_remote_copy(
        src_ref=src,
        dst_ref=dst,
        send_sem=send_sem,
        recv_sem=recv_sem,
        device_id=device,
        device_id_type=MESH,
    )
    copy.start()
    return copy


def batches(ring):
    half = ring // 2
    return [(0, 1)] + [(2 * d - 1, 2) for d in range(1, half)] + [(ring - 1, 1)]


def spread(count):
    return (count // 8 | 1) * 8


def rows_at(index, count):
    return pl.ds(pl.multiple_of(index * count, count), count)


def chooser(pick_row, images, length):
    shape = (images * length, pick_row.shape[1])
    row = lax.broadcasted_iota(jnp.int32, shape, 0)
    column = lax.broadcasted_iota(jnp.int32, shape, 1)
    image = lax.div(row, length).astype(jnp.float32)
    same = lax.rem(row, length) == lax.rem(column, length)
    return jnp.where(same & (image == pick_row), 1.0, 0.0).astype(jnp.bfloat16)


def gather_kernel(
    grid,
    ring_z,
    steps_y,
    steps_z,
    images,
    length,
    picks_arg,
    tokens_arg,
    weight_arg,
    grads_arg,
    firsts_arg,
    seconds_arg,
    pool,
    received,
    laid,
    firsts,
    places,
    pick_rows,
    feature,
    picks,
    tokens,
    weight,
    grads,
    seconds,
    blocks,
    stage,
    fetch_sem,
    y_send,
    y_recv,
    z_send,
    z_recv,
    x_send,
    x_recv,
):
    here = Where(grid, ring_z)
    ring_y, peers = here.ring_y, here.peers
    rows, width = tokens.shape
    block_rows = blocks.shape[1]
    fetches = [
        pltpu.make_async_copy(src, dst, fetch_sem.at[n])
        for n, (src, dst) in enumerate(
            (
                (tokens_arg, tokens),
                (weight_arg, weight),
                (picks_arg, picks),
                (seconds_arg, seconds),
                (firsts_arg, firsts),
                (grads_arg, grads),
            )
        )
    ]
    for fetch in fetches:
        fetch.start()
    met = here.greet(steps_y, steps_z)

    for fetch in fetches[:3]:
        fetch.wait()
    projected = jnp.dot(tokens[...], weight[...], preferred_element_type=jnp.float32)
    feature[...] = projected
    mean_square = jnp.mean(projected * projected, axis=-1, keepdims=True)
    normed = (projected * lax.rsqrt(mean_square + EPSILON)).astype(jnp.bfloat16)
    blocks[0, :rows] = normed
    pool[here.z] = normed
    tail = (block_rows - rows, peers * length)
    tail_row = lax.broadcasted_iota(jnp.int32, tail, 0)
    tail_peer = lax.div(lax.broadcasted_iota(jnp.int32, tail, 1), length)
    table = jnp.zeros(tail, jnp.int32)
    for y in range(ring_y):
        for s in range(peers):
            slot = (s // here.cores * ring_y + y) * here.cores + s % here.cores
            table = jnp.where((tail_row == y) & (tail_peer == s), picks[slot], table)
    blocks[0, rows:] = table.astype(jnp.float32).astype(jnp.bfloat16)
    met()

    half_y, half_z = ring_y // 2, ring_z // 2
    y_copies, z_copies, x_copies = {}, {}, []

    def forward_y(source):
        for distance, before in steps_y.items():
            if before != source:
                continue
            for way, turn in enumerate((1, -1)):
                part = pl.ds(0, block_rows)
                if distance == half_y:
                    part = pl.ds(0, rows // 2) if way == 0 else pl.ds(rows // 2, block_rows - rows // 2)
                y_copies[distance, way] = send(
                    blocks.at[place_of(-turn * before, ring_y), part],
                    blocks.at[place_of(-turn * distance, ring_y), part],
                    y_send.at[way, distance - 1],
                    y_recv.at[way, distance - 1],
                    here.along_y(turn * (distance - before)),
                )

    def forward_z(source):
        for distance, before in steps_z.items():
            if before != source:
                continue
            for way, turn in enumerate((1, -1)):
                part = pl.ds(way * (rows // 2), rows // 2) if distance == half_z else pl.ds(0, rows)
                owner = here.z_at(-turn * before)
                z_copies[distance, way] = send(
                    pool.at[owner, part],
                    pool.at[owner, part],
                    z_send.at[way, distance - 1],
                    z_recv.at[way, distance - 1],
                    here.along_z(turn * (distance - before)),
                )

    own = rows_at(here.s, length)

    def choose(batch, place, count):
        for at in range(place, place + count):
            rows_of_y = blocks[at, rows:].astype(jnp.float32)
            mine = jnp.sum(jnp.where(tail_row == here.y, rows_of_y, 0.0), axis=0, keepdims=True)
            pick_rows[at] = jnp.broadcast_to(mine, pick_rows.shape[1:])
            stage[at] = lax.dot_general(
                chooser(mine, images, length),
                blocks[at, :rows],
                (((0,), (0,)), ((), ())),
                preferred_element_type=jnp.float32,
            ).astype(jnp.bfloat16)
        for turn in range(1, peers):
            x_copies.append(
                send(
                    stage.at[pl.ds(place, count), rows_at(here.s_at(turn), length)],
                    received.at[pl.ds(place, count), own],
                    x_send.at[batch, turn - 1],
                    x_recv.at[batch, turn - 1],
                    here.across(turn),
                )
            )
        for at in range(place, place + count):
            received[at, own] = stage[at, own]

    forward_y(0)
    forward_z(0)
    plan = batches(ring_y)
    choose(0, *plan[0])
    for fetch in fetches[3:]:
        fetch.wait()

    slot = seconds[...]
    offset = lax.rem(lax.rem(lax.div(slot, here.cores), ring_y) - here.y + ring_y, ring_y)
    near = jnp.where(2 * offset <= ring_y, 2 * offset - 1, 2 * (ring_y - offset))
    place = jnp.where(offset == 0, 0, near)
    peer = lax.div(slot, here.cores * ring_y) * here.cores + lax.rem(slot, here.cores)
    places[...] = place * peers + peer

    across = LANES // length
    groups = grads.shape[0] // across
    lane_block = lax.div(lax.broadcasted_iota(jnp.int32, (groups, LANES), 1), length)

    def lay(tile):
        wide = grads[:, tile * LANES : (tile + 1) * LANES].astype(jnp.float32)
        parts = [wide[q * groups : (q + 1) * groups] for q in range(across)]
        for r in range(across):
            total = None
            for q in range(across):
                shift = (q - r) % across * length
                moved = pltpu.roll(parts[q], shift, 1) if shift else parts[q]
                total = moved if total is None else jnp.where(lane_block == q, moved, total)
            i = tile * across + r
            laid[i * spread(groups) : i * spread(groups) + groups] = total

    tiles = grads.shape[1] // LANES
    todo = list(range(tiles))
    for distance in range(1, max(half_y, half_z) + 1):
        if todo:
            lay(todo.pop(0))
        if distance <= half_y:
            for way in range(2):
                y_copies[distance, way].wait_recv()
            forward_y(distance)
        if distance <= half_z:
            for way in range(2):
                z_copies[distance, way].wait_recv()
            forward_z(distance)
        if distance <= half_y:
            choose(distance, *plan[distance])
    for tile in todo:
        lay(tile)
    for copy in x_copies:
        copy.wait_recv()
    for copy in [*y_copies.values(), *z_copies.values(), *x_copies]:
        copy.wait_send()


def pair_gradients(length, first_ref, place_ref, pool, received, laid, by_first, by_second):
    pairs = first_ref.shape[1]
    across = LANES // length
    groups = pairs // across
    width = pool.shape[2]
    scale = 1.0 / (width * SOFTMAX_COOLING)
    together = min(8, groups)

    side = (LANES, LANES)
    row_block = lax.div(lax.broadcasted_iota(jnp.int32, side, 0), length)
    lane_block = lax.div(lax.broadcasted_iota(jnp.int32, side, 1), length)
    diagonal = row_block == lane_block
    ones = jnp.where(diagonal, 1.0, 0.0).astype(jnp.bfloat16)
    ones = jnp.concatenate([ones, ones], axis=0)
    narrow = lax.div(lax.broadcasted_iota(jnp.int32, (length, LANES), 1), length)

    def block_sums(values):
        high = values.astype(jnp.bfloat16)
        low = (values - high.astype(jnp.float32)).astype(jnp.bfloat16)
        return jnp.dot(
            jnp.concatenate([high, low], axis=1), ones, preferred_element_type=jnp.float32
        )

    def step(chunk, carry):
        firsts, seconds, scores, incoming = [], [], [], []
        for n in range(together):
            g = chunk * together + n
            pairs_of_g = [q * groups + g for q in range(across)]
            firsts.append(jnp.concatenate([pool[first_ref[0, e]] for e in pairs_of_g], axis=0))
            seconds.append(jnp.concatenate([received[place_ref[0, e]] for e in pairs_of_g], axis=0))
            full = lax.dot_general(
                firsts[n],
                seconds[n],
                (((1,), (1,)), ((), ())),
                preferred_element_type=jnp.float32,
            )
            packed = full[:length]
            for q in range(1, across):
                packed = jnp.where(narrow == q, full[q * length : (q + 1) * length], packed)
            scores.append(packed)
            incoming.append(laid[pl.ds(g, length, stride=spread(groups)), :])
        shape = (together, length, LANES)
        expo = jnp.exp(jnp.concatenate(scores, axis=0) * scale)
        gradient = jnp.concatenate(incoming, axis=0)
        rows = expo / block_sums(expo)
        expo = expo.reshape(shape)
        cols = (expo / jnp.sum(expo, axis=1, keepdims=True)).reshape(rows.shape)
        both = gradient * rows * cols
        over_second = block_sums(both)
        over_first = jnp.sum(both.reshape(shape), axis=1, keepdims=True)
        part = (cols.reshape(shape) * over_first).reshape(rows.shape)
        d_scaled = ((2.0 * both - rows * over_second - part) * scale).astype(jnp.bfloat16)
        for n in range(together):
            mine = d_scaled[n * length : (n + 1) * length]
            wide = jnp.concatenate([mine] * across, axis=0)
            wide = jnp.where(diagonal, wide, jnp.zeros_like(wide))
            grad_first = jnp.dot(wide, seconds[n], preferred_element_type=jnp.float32)
            grad_second = lax.dot_general(
                wide, firsts[n], (((0,), (0,)), ((), ())), preferred_element_type=jnp.float32
            )
            for q in range(across):
                part = slice(q * length, (q + 1) * length)
                rows_of_pair = pl.ds(q * groups + chunk * together + n, length, stride=spread(pairs))
                for h in range(width // LANES):
                    lanes = slice(h * LANES, (h + 1) * LANES)
                    by_first[h, rows_of_pair, :] = grad_first[part, lanes]
                    by_second[h, rows_of_pair, :] = grad_second[part, lanes]
        return carry

    lax.fori_loop(0, groups // together, step, 0)


def add_up(length, image_of_pair, by_pair, total, rounded):
    pairs = image_of_pair.shape[1]
    far = spread(length)
    halves, count = total.shape[0], total.shape[1] // far
    image = lax.broadcasted_iota(jnp.int32, (count, pairs), 0)
    chosen = jnp.where(image == image_of_pair[...], 1.0, 0.0).astype(jnp.bfloat16)
    together = length

    def step(chunk, carry):
        for n in range(together):
            i = chunk * together + n
            rows_of_i = pl.ds(pl.multiple_of(i * spread(pairs), 8), pairs)
            rows_of_i = [by_pair[h, rows_of_i].astype(jnp.bfloat16) for h in range(halves)]
            sums = jnp.dot(
                chosen, jnp.concatenate(rows_of_i, axis=1), preferred_element_type=jnp.float32
            )
            for h in range(halves):
                lanes = slice(h * LANES, (h + 1) * LANES)
                total[h, pl.ds(i, count, stride=far), :] = sums[:, lanes]
        return carry

    lax.fori_loop(0, length // together, step, 0)
    images = rounded.shape[1] // length
    for n in range(count):
        rows_of_image = slice(n % images * length, (n % images + 1) * length)
        for h in range(halves):
            rounded[n // images, rows_of_image, h * LANES : (h + 1) * LANES] = total[
                h, n * far : n * far + length
            ].astype(jnp.bfloat16)


def return_kernel(
    grid,
    ring_z,
    steps_y,
    steps_z,
    images,
    length,
    first_ref,
    place_ref,
    firsts,
    places,
    pool_images,
    received,
    laid,
    pick_rows,
    feature,
    feature_grad,
    by_first,
    by_second,
    pool_total,
    slot_total,
    slots,
    pool,
    arrived,
    choosers,
    y_in,
    y_out,
    z_in,
    z_out,
    y_send,
    y_recv,
    z_send,
    z_recv,
    x_send,
    x_recv,
):
    here = Where(grid, ring_z)
    ring_y, peers = here.ring_y, here.peers
    rows, width = feature.shape
    half_y, half_z = ring_y // 2, ring_z // 2
    met = here.greet(steps_y, steps_z)
    own = rows_at(here.s, length)
    plan = batches(ring_y)
    pair_gradients(
        length, first_ref, place_ref, pool_images, received, laid, by_first, by_second
    )
    add_up(length, firsts, by_first, pool_total, pool)
    met()

    y_copies, z_copies, x_copies = {}, {}, {}

    def part_of(distance, way, half):
        return pl.ds(way * (rows // 2), rows // 2) if distance == half else pl.ds(0, rows)

    def send_z(distance):
        hop = distance - steps_z[distance]
        for way, turn in enumerate((1, -1)):
            part = part_of(distance, way, half_z)
            if distance in steps_z.values():
                source = z_out.at[way, distance - 1, part]
            else:
                source = pool.at[here.z_at(turn * distance), part]
            z_copies[distance, way] = send(
                source,
                z_in.at[way, distance - 1, part],
                z_send.at[way, distance - 1],
                z_recv.at[way, distance - 1],
                here.along_z(turn * hop),
            )

    def send_y(distance):
        hop = distance - steps_y[distance]
        for way, turn in enumerate((1, -1)):
            part = part_of(distance, way, half_y)
            y_copies[distance, way] = send(
                y_out.at[way, distance - 1, part],
                y_in.at[way, distance - 1, part],
                y_send.at[way, distance - 1],
                y_recv.at[way, distance - 1],
                here.along_y(turn * hop),
            )

    for distance in range(half_z, 0, -1):
        if distance not in steps_z.values():
            send_z(distance)
    add_up(length, places, by_second, slot_total, slots)
    for distance in range(half_y, -1, -1):
        place, count = plan[distance]
        x_copies[distance] = [
            send(
                slots.at[pl.ds(place, count), rows_at(here.s_at(turn), length)],
                arrived.at[pl.ds(place, count), own],
                x_send.at[distance, turn - 1],
                x_recv.at[distance, turn - 1],
                here.across(turn),
            )
            for turn in range(1, peers)
        ]
    for at in range(ring_y):
        arrived[at, own] = slots[at, own]
        choosers[at] = chooser(pick_rows[at, :1], images, length)

    def summed(place):
        return jnp.dot(choosers[place], arrived[place], preferred_element_type=jnp.float32)

    def wait_x(distance):
        for copy in x_copies[distance]:
            copy.wait_recv()

    def joined(total, ins, way, distance, half):
        if distance < half:
            return total + ins[way, distance - 1].astype(jnp.float32)
        low = way * (rows // 2)
        added = ins[way, distance - 1, low : low + rows // 2].astype(jnp.float32)
        added = added + total[low : low + rows // 2]
        rest = total[rows // 2 :] if way == 0 else total[: rows // 2]
        return jnp.concatenate([added, rest] if way == 0 else [rest, added], axis=0)

    def collect(total, way, distance, steps, copies, ins, half):
        for farther in sorted(steps, reverse=True):
            if steps[farther] == distance:
                copies[farther, way].wait_recv()
                total = joined(total, ins, way, farther, half)
        return total

    along_z = (steps_z, z_copies, z_in, half_z)
    along_y = (steps_y, y_copies, y_in, half_y)
    for distance in range(max(half_y, half_z), 0, -1):
        if distance <= half_y:
            wait_x(distance)
            for way, turn in enumerate((1, -1)):
                if distance < half_y or way == 0:
                    mine = summed(place_of(turn * distance, ring_y))
                total = collect(mine, way, distance, *along_y)
                y_out[way, distance - 1] = total.astype(jnp.bfloat16)
            send_y(distance)
        if distance <= half_z and distance in steps_z.values():
            for way, turn in enumerate((1, -1)):
                mine = pool[here.z_at(turn * distance)].astype(jnp.float32)
                total = collect(mine, way, distance, *along_z)
                z_out[way, distance - 1] = total.astype(jnp.bfloat16)
            send_z(distance)
    wait_x(0)
    gradient = summed(0) + pool[here.z].astype(jnp.float32)
    projected = feature[...]
    mean_square = jnp.mean(projected * projected, axis=-1, keepdims=True)
    inv_rms = lax.rsqrt(mean_square + EPSILON)
    normed = projected * inv_rms
    for way in range(2):
        gradient = collect(gradient, way, 0, *along_z)
        gradient = collect(gradient, way, 0, *along_y)
    mean = jnp.mean(gradient * normed, axis=-1, keepdims=True)
    feature_grad[...] = (inv_rms * (gradient - normed * mean)).astype(jnp.bfloat16)
    for copy in [*y_copies.values(), *z_copies.values(), *sum(x_copies.values(), [])]:
        copy.wait_send()


def in_vmem(count):
    return [pl.BlockSpec(memory_space=pltpu.VMEM)] * count


def in_smem(count):
    return [pl.BlockSpec(memory_space=pltpu.SMEM)] * count


def ring_semaphores(half_y, half_z, peers):
    dma = pltpu.SemaphoreType.DMA
    pairs = [(2, half_y), (2, half_z), (half_y + 1, peers - 1)]
    return [dma(shape) for shape in pairs for _ in range(2)]


def local(
    grid,
    ring_z,
    steps_y,
    steps_z,
    tokens,
    proj_weight,
    match_grad,
    edge_first,
    pair_second_image,
    send_pick,
):
    images, length, width = tokens.shape
    rows = images * length
    pairs = edge_first.shape[0]
    ring_y, peers = grid[1], grid[0] * grid[2]
    half_y, half_z = ring_y // 2, ring_z // 2
    layout = (grid, ring_z, steps_y, steps_z, images, length)
    bf16, f32 = jnp.bfloat16, jnp.float32
    shape = jax.ShapeDtypeStruct
    pool_rows, slot_rows = ring_z * rows, ring_y * peers * length

    pool, received, laid, firsts, places, pick_rows, feature = pl.pallas_call(
        functools.partial(gather_kernel, *layout),
        out_shape=(
            shape((ring_z, rows, width), bf16),
            shape((ring_y, peers * length, width), bf16),
            shape((length * spread(pairs * length // LANES), LANES), f32),
            shape((1, pairs), jnp.int32),
            shape((1, pairs), jnp.int32),
            shape((ring_y, 8, peers * length), f32),
            shape((rows, width), f32),
        ),
        in_specs=[pl.BlockSpec(memory_space=pltpu.HBM)] * 6,
        out_specs=tuple(in_vmem(7)),
        scratch_shapes=[
            pltpu.SMEM((send_pick.shape[0],), jnp.int32),
            pltpu.VMEM((rows, width), bf16),
            pltpu.VMEM(proj_weight.shape, bf16),
            pltpu.VMEM(match_grad.shape, bf16),
            pltpu.VMEM((1, pairs), jnp.int32),
            pltpu.VMEM((ring_y, rows + 16, width), bf16),
            pltpu.VMEM((ring_y, peers * length, width), bf16),
            pltpu.SemaphoreType.DMA((6,)),
            *ring_semaphores(half_y, half_z, peers),
        ],
        compiler_params=pltpu.CompilerParams(
            collective_id=0, has_side_effects=True, vmem_limit_bytes=VMEM_LIMIT
        ),
        name="gather_images",
    )(
        *(
            pltpu.with_memory_space_constraint(argument, pltpu.HBM)
            for argument in (
                send_pick,
                tokens.reshape(rows, width),
                proj_weight,
                match_grad,
                edge_first.reshape(1, pairs),
                pair_second_image.reshape(1, pairs),
            )
        )
    )

    feature_grad = pl.pallas_call(
        functools.partial(return_kernel, *layout),
        out_shape=shape((rows, width), bf16),
        in_specs=in_smem(2) + in_vmem(7),
        out_specs=pl.BlockSpec(memory_space=pltpu.VMEM),
        scratch_shapes=[
            pltpu.VMEM((width // LANES, length * spread(pairs), LANES), f32),
            pltpu.VMEM((width // LANES, length * spread(pairs), LANES), f32),
            pltpu.VMEM((width // LANES, pool_rows // length * spread(length), LANES), f32),
            pltpu.VMEM((width // LANES, slot_rows // length * spread(length), LANES), f32),
            pltpu.VMEM((ring_y, peers * length, width), bf16),
            pltpu.VMEM((ring_z, rows, width), bf16),
            pltpu.VMEM((ring_y, peers * length, width), bf16),
            pltpu.VMEM((ring_y, rows, peers * length), bf16),
            pltpu.VMEM((2, half_y, rows, width), bf16),
            pltpu.VMEM((2, half_y, rows, width), bf16),
            pltpu.VMEM((2, half_z, rows, width), bf16),
            pltpu.VMEM((2, half_z, rows, width), bf16),
            *ring_semaphores(half_y, half_z, peers),
        ],
        compiler_params=pltpu.CompilerParams(
            collective_id=1, has_side_effects=True, vmem_limit_bytes=VMEM_LIMIT
        ),
        name="return_gradients",
    )(
        firsts,
        places,
        firsts,
        places,
        pool.reshape(pool_rows // length, length, width),
        received.reshape(slot_rows // length, length, width),
        laid,
        pick_rows,
        feature,
    )
    token_grad = lax.dot_general(
        feature_grad, proj_weight, (((1,), (1,)), ((), ())), preferred_element_type=f32
    )
    return token_grad.astype(bf16).reshape(images, length, width)


def solution(mesh, grid=GRID, steps_y=STEPS_Y, steps_z=STEPS_Z):
    placed = (
        P(("grp", "sub"), None, None),
        P(),
        P(("grp", "sub"), None),
        P(("grp", "sub")),
        P(("grp", "sub")),
        P(("grp", "sub")),
    )
    return jax.shard_map(
        functools.partial(local, grid, mesh.shape["sub"], steps_y, steps_z),
        mesh=mesh,
        in_specs=placed,
        out_specs=P(("grp", "sub"), None, None),
        check_vma=False,
    )
```

```python
import functools

import jax
import jax.numpy as jnp
from jax import lax
from jax.experimental import pallas as pl
from jax.experimental.pallas import tpu as pltpu
from jax.sharding import PartitionSpec as P

EPSILON = 1e-05
SOFTMAX_COOLING = 0.1
MESH = pl.DeviceIdType.MESH
LANES = 128
VMEM_LIMIT = 40 * 1024 * 1024
GRID = (4, 8, 2)
STEPS_Y = {1: 0, 2: 0, 3: 1, 4: 2}
STEPS_Z = {2: 0, 1: 0, 4: 2, 3: 2, 6: 4, 5: 4}
ARRIVALS = "y1 z2 y2 z1 z4 y3 y4 z3 z6 z5"


def place_of(offset, ring):
    offset %= ring
    return 0 if offset == 0 else 2 * offset - 1 if 2 * offset <= ring else 2 * (ring - offset)


class Where:
    def __init__(self, grid, ring_z):
        _, self.ring_y, cores = grid
        self.cores, self.ring_z, self.peers = cores, ring_z, grid[0] * cores
        grp = lax.axis_index("grp")
        self.z = lax.axis_index("sub")
        self.y = lax.rem(lax.div(grp, cores), self.ring_y)
        self.s = lax.div(grp, cores * self.ring_y) * cores + lax.rem(grp, cores)

    def group(self, s, y):
        return (lax.div(s, self.cores) * self.ring_y + y) * self.cores + lax.rem(s, self.cores)

    def along_y(self, step):
        return {"grp": self.group(self.s, lax.rem(self.y + step + self.ring_y, self.ring_y))}

    def z_at(self, step):
        return lax.rem(self.z + step + self.ring_z, self.ring_z)

    def along_z(self, step):
        return {"sub": self.z_at(step)}

    def s_at(self, turn):
        return lax.rem(self.s + turn, self.peers)

    def across(self, turn):
        return {"grp": self.group(self.s_at(turn), self.y)}

    def greet(self, steps_y, steps_z):
        barrier = pltpu.get_barrier_semaphore()
        others = []
        for hop in sorted({distance - before for distance, before in steps_y.items()}):
            others += [self.along_y(hop), self.along_y(-hop)]
        for hop in sorted({distance - before for distance, before in steps_z.items()}):
            others += [self.along_z(hop), self.along_z(-hop)]
        others += [self.across(turn) for turn in range(1, self.peers)]
        for other in others:
            pl.semaphore_signal(barrier, inc=1, device_id=other, device_id_type=MESH)
        return lambda: pl.semaphore_wait(barrier, len(others))


def send(src, dst, send_sem, recv_sem, device):
    copy = pltpu.make_async_remote_copy(
        src_ref=src,
        dst_ref=dst,
        send_sem=send_sem,
        recv_sem=recv_sem,
        device_id=device,
        device_id_type=MESH,
    )
    copy.start()
    return copy


def batches(ring):
    half = ring // 2
    return [(0, 1)] + [(2 * d - 1, 2) for d in range(1, half)] + [(ring - 1, 1)]


def spread(count):
    return (count // 8 | 1) * 8


def rows_at(index, count):
    return pl.ds(pl.multiple_of(index * count, count), count)


def chooser(pick_row, images, length):
    shape = (images * length, pick_row.shape[1])
    row = lax.broadcasted_iota(jnp.int32, shape, 0)
    column = lax.broadcasted_iota(jnp.int32, shape, 1)
    image = lax.div(row, length).astype(jnp.float32)
    same = lax.rem(row, length) == lax.rem(column, length)
    return jnp.where(same & (image == pick_row), 1.0, 0.0).astype(jnp.bfloat16)


def gather_kernel(
    grid,
    ring_z,
    steps_y,
    steps_z,
    images,
    length,
    picks_arg,
    tokens_arg,
    weight_arg,
    grads_arg,
    firsts_arg,
    seconds_arg,
    pool,
    received,
    laid,
    firsts,
    places,
    pick_rows,
    feature,
    picks,
    tokens,
    weight,
    grads,
    seconds,
    blocks,
    stage,
    fetch_sem,
    y_send,
    y_recv,
    z_send,
    z_recv,
    x_send,
    x_recv,
):
    here = Where(grid, ring_z)
    ring_y, peers = here.ring_y, here.peers
    rows, width = tokens.shape
    block_rows = blocks.shape[1]
    fetches = [
        pltpu.make_async_copy(src, dst, fetch_sem.at[n])
        for n, (src, dst) in enumerate(
            (
                (tokens_arg, tokens),
                (weight_arg, weight),
                (picks_arg, picks),
                (seconds_arg, seconds),
                (firsts_arg, firsts),
                (grads_arg, grads),
            )
        )
    ]
    for fetch in fetches:
        fetch.start()
    met = here.greet(steps_y, steps_z)

    for fetch in fetches[:3]:
        fetch.wait()
    projected = jnp.dot(tokens[...], weight[...], preferred_element_type=jnp.float32)
    feature[...] = projected
    mean_square = jnp.mean(projected * projected, axis=-1, keepdims=True)
    normed = (projected * lax.rsqrt(mean_square + EPSILON)).astype(jnp.bfloat16)
    blocks[0, :rows] = normed
    pool[here.z] = normed
    tail = (block_rows - rows, peers * length)
    tail_row = lax.broadcasted_iota(jnp.int32, tail, 0)
    tail_peer = lax.div(lax.broadcasted_iota(jnp.int32, tail, 1), length)
    table = jnp.zeros(tail, jnp.int32)
    for y in range(ring_y):
        for s in range(peers):
            slot = (s // here.cores * ring_y + y) * here.cores + s % here.cores
            table = jnp.where((tail_row == y) & (tail_peer == s), picks[slot], table)
    blocks[0, rows:] = table.astype(jnp.float32).astype(jnp.bfloat16)
    met()

    half_y, half_z = ring_y // 2, ring_z // 2
    y_copies, z_copies, x_copies = {}, {}, []

    def forward_y(source):
        for distance, before in steps_y.items():
            if before != source:
                continue
            for way, turn in enumerate((1, -1)):
                part = pl.ds(0, block_rows)
                if distance == half_y:
                    part = pl.ds(0, rows // 2) if way == 0 else pl.ds(rows // 2, block_rows - rows // 2)
                y_copies[distance, way] = send(
                    blocks.at[place_of(-turn * before, ring_y), part],
                    blocks.at[place_of(-turn * distance, ring_y), part],
                    y_send.at[way, distance - 1],
                    y_recv.at[way, distance - 1],
                    here.along_y(turn * (distance - before)),
                )

    def forward_z(source):
        for distance, before in steps_z.items():
            if before != source:
                continue
            for way, turn in enumerate((1, -1)):
                part = pl.ds(way * (rows // 2), rows // 2) if distance == half_z else pl.ds(0, rows)
                owner = here.z_at(-turn * before)
                z_copies[distance, way] = send(
                    pool.at[owner, part],
                    pool.at[owner, part],
                    z_send.at[way, distance - 1],
                    z_recv.at[way, distance - 1],
                    here.along_z(turn * (distance - before)),
                )

    own = rows_at(here.s, length)

    def choose(batch, place, count):
        for at in range(place, place + count):
            rows_of_y = blocks[at, rows:].astype(jnp.float32)
            mine = jnp.sum(jnp.where(tail_row == here.y, rows_of_y, 0.0), axis=0, keepdims=True)
            pick_rows[at] = jnp.broadcast_to(mine, pick_rows.shape[1:])
            stage[at] = lax.dot_general(
                chooser(mine, images, length),
                blocks[at, :rows],
                (((0,), (0,)), ((), ())),
                preferred_element_type=jnp.float32,
            ).astype(jnp.bfloat16)
        for turn in range(1, peers):
            x_copies.append(
                send(
                    stage.at[pl.ds(place, count), rows_at(here.s_at(turn), length)],
                    received.at[pl.ds(place, count), own],
                    x_send.at[batch, turn - 1],
                    x_recv.at[batch, turn - 1],
                    here.across(turn),
                )
            )
        for at in range(place, place + count):
            received[at, own] = stage[at, own]

    forward_y(0)
    forward_z(0)
    plan = batches(ring_y)
    choose(0, *plan[0])
    for fetch in fetches[3:]:
        fetch.wait()

    slot = seconds[...]
    offset = lax.rem(lax.rem(lax.div(slot, here.cores), ring_y) - here.y + ring_y, ring_y)
    near = jnp.where(2 * offset <= ring_y, 2 * offset - 1, 2 * (ring_y - offset))
    place = jnp.where(offset == 0, 0, near)
    peer = lax.div(slot, here.cores * ring_y) * here.cores + lax.rem(slot, here.cores)
    places[...] = place * peers + peer

    across = LANES // length
    groups = grads.shape[0] // across
    lane_block = lax.div(lax.broadcasted_iota(jnp.int32, (groups, LANES), 1), length)

    def lay(tile):
        wide = grads[:, tile * LANES : (tile + 1) * LANES].astype(jnp.float32)
        parts = [wide[q * groups : (q + 1) * groups] for q in range(across)]
        for r in range(across):
            total = None
            for q in range(across):
                shift = (q - r) % across * length
                moved = pltpu.roll(parts[q], shift, 1) if shift else parts[q]
                total = moved if total is None else jnp.where(lane_block == q, moved, total)
            i = tile * across + r
            laid[i * spread(groups) : i * spread(groups) + groups] = total

    tiles = grads.shape[1] // LANES
    todo = list(range(tiles))
    for arrival in ARRIVALS.split():
        axis, distance = arrival[0], int(arrival[1:])
        if todo:
            lay(todo.pop(0))
        if axis == "y" and distance <= half_y:
            for way in range(2):
                y_copies[distance, way].wait_recv()
            forward_y(distance)
            choose(distance, *plan[distance])
        if axis == "z" and distance <= half_z:
            for way in range(2):
                z_copies[distance, way].wait_recv()
            forward_z(distance)
    for tile in todo:
        lay(tile)
    for copy in x_copies:
        copy.wait_recv()
    for copy in [*y_copies.values(), *z_copies.values(), *x_copies]:
        copy.wait_send()


def pair_gradients(length, first_ref, place_ref, pool, received, laid, by_first, by_second):
    pairs = first_ref.shape[1]
    across = LANES // length
    groups = pairs // across
    width = pool.shape[2]
    scale = 1.0 / (width * SOFTMAX_COOLING)
    together = groups

    side = (LANES, LANES)
    row_block = lax.div(lax.broadcasted_iota(jnp.int32, side, 0), length)
    lane_block = lax.div(lax.broadcasted_iota(jnp.int32, side, 1), length)
    diagonal = row_block == lane_block
    ones = jnp.where(diagonal, 1.0, 0.0).astype(jnp.bfloat16)
    ones = jnp.concatenate([ones, ones], axis=0)
    narrow = lax.div(lax.broadcasted_iota(jnp.int32, (length, LANES), 1), length)

    def block_sums(values):
        high = values.astype(jnp.bfloat16)
        low = (values - high.astype(jnp.float32)).astype(jnp.bfloat16)
        return jnp.dot(
            jnp.concatenate([high, low], axis=1), ones, preferred_element_type=jnp.float32
        )

    def step(chunk, carry):
        firsts, seconds, scores, incoming = [], [], [], []
        for n in range(together):
            g = chunk * together + n
            pairs_of_g = [q * groups + g for q in range(across)]
            firsts.append(jnp.concatenate([pool[first_ref[0, e]] for e in pairs_of_g], axis=0))
            seconds.append(jnp.concatenate([received[place_ref[0, e]] for e in pairs_of_g], axis=0))
            full = lax.dot_general(
                firsts[n],
                seconds[n],
                (((1,), (1,)), ((), ())),
                preferred_element_type=jnp.float32,
            )
            packed = full[:length]
            for q in range(1, across):
                packed = jnp.where(narrow == q, full[q * length : (q + 1) * length], packed)
            scores.append(packed)
            incoming.append(laid[pl.ds(g, length, stride=spread(groups)), :])
        shape = (together, length, LANES)
        expo = jnp.exp(jnp.concatenate(scores, axis=0) * scale)
        gradient = jnp.concatenate(incoming, axis=0)
        rows = expo / block_sums(expo)
        expo = expo.reshape(shape)
        cols = (expo / jnp.sum(expo, axis=1, keepdims=True)).reshape(rows.shape)
        both = gradient * rows * cols
        over_second = block_sums(both)
        over_first = jnp.sum(both.reshape(shape), axis=1, keepdims=True)
        part = (cols.reshape(shape) * over_first).reshape(rows.shape)
        d_scaled = ((2.0 * both - rows * over_second - part) * scale).astype(jnp.bfloat16)
        for n in range(together):
            mine = d_scaled[n * length : (n + 1) * length]
            wide = jnp.concatenate([mine] * across, axis=0)
            wide = jnp.where(diagonal, wide, jnp.zeros_like(wide))
            grad_first = jnp.dot(wide, seconds[n], preferred_element_type=jnp.float32)
            grad_second = lax.dot_general(
                wide, firsts[n], (((0,), (0,)), ((), ())), preferred_element_type=jnp.float32
            )
            for q in range(across):
                part = slice(q * length, (q + 1) * length)
                rows_of_pair = pl.ds(q * groups + chunk * together + n, length, stride=spread(pairs))
                for h in range(width // LANES):
                    lanes = slice(h * LANES, (h + 1) * LANES)
                    by_first[h, rows_of_pair, :] = grad_first[part, lanes]
                    by_second[h, rows_of_pair, :] = grad_second[part, lanes]
        return carry

    lax.fori_loop(0, groups // together, step, 0)


def add_up(length, image_of_pair, by_pair, total, rounded):
    pairs = image_of_pair.shape[1]
    far = spread(length)
    halves, count = total.shape[0], total.shape[1] // far
    image = lax.broadcasted_iota(jnp.int32, (count, pairs), 0)
    chosen = jnp.where(image == image_of_pair[...], 1.0, 0.0).astype(jnp.bfloat16)
    together = length

    def step(chunk, carry):
        for n in range(together):
            i = chunk * together + n
            rows_of_i = pl.ds(pl.multiple_of(i * spread(pairs), 8), pairs)
            rows_of_i = [by_pair[h, rows_of_i].astype(jnp.bfloat16) for h in range(halves)]
            sums = jnp.dot(
                chosen, jnp.concatenate(rows_of_i, axis=1), preferred_element_type=jnp.float32
            )
            for h in range(halves):
                lanes = slice(h * LANES, (h + 1) * LANES)
                total[h, pl.ds(i, count, stride=far), :] = sums[:, lanes]
        return carry

    lax.fori_loop(0, length // together, step, 0)
    images = rounded.shape[1] // length
    for n in range(count):
        rows_of_image = slice(n % images * length, (n % images + 1) * length)
        for h in range(halves):
            rounded[n // images, rows_of_image, h * LANES : (h + 1) * LANES] = total[
                h, n * far : n * far + length
            ].astype(jnp.bfloat16)


def return_kernel(
    grid,
    ring_z,
    steps_y,
    steps_z,
    images,
    length,
    first_ref,
    place_ref,
    firsts,
    places,
    pool_images,
    received,
    laid,
    pick_rows,
    feature,
    feature_grad,
    by_first,
    by_second,
    pool_total,
    slot_total,
    slots,
    pool,
    arrived,
    choosers,
    y_in,
    y_out,
    z_in,
    z_out,
    y_send,
    y_recv,
    z_send,
    z_recv,
    x_send,
    x_recv,
):
    here = Where(grid, ring_z)
    ring_y, peers = here.ring_y, here.peers
    rows, width = feature.shape
    half_y, half_z = ring_y // 2, ring_z // 2
    met = here.greet(steps_y, steps_z)
    own = rows_at(here.s, length)
    plan = batches(ring_y)
    pair_gradients(
        length, first_ref, place_ref, pool_images, received, laid, by_first, by_second
    )
    add_up(length, places, by_second, slot_total, slots)
    met()

    y_copies, z_copies, x_copies = {}, {}, {}

    def part_of(distance, way, half):
        return pl.ds(way * (rows // 2), rows // 2) if distance == half else pl.ds(0, rows)

    def send_z(distance):
        hop = distance - steps_z[distance]
        for way, turn in enumerate((1, -1)):
            part = part_of(distance, way, half_z)
            if distance in steps_z.values():
                source = z_out.at[way, distance - 1, part]
            else:
                source = pool.at[here.z_at(turn * distance), part]
            z_copies[distance, way] = send(
                source,
                z_in.at[way, distance - 1, part],
                z_send.at[way, distance - 1],
                z_recv.at[way, distance - 1],
                here.along_z(turn * hop),
            )

    def send_y(distance):
        hop = distance - steps_y[distance]
        for way, turn in enumerate((1, -1)):
            part = part_of(distance, way, half_y)
            y_copies[distance, way] = send(
                y_out.at[way, distance - 1, part],
                y_in.at[way, distance - 1, part],
                y_send.at[way, distance - 1],
                y_recv.at[way, distance - 1],
                here.along_y(turn * hop),
            )

    for distance in range(half_y, -1, -1):
        place, count = plan[distance]
        x_copies[distance] = [
            send(
                slots.at[pl.ds(place, count), rows_at(here.s_at(turn), length)],
                arrived.at[pl.ds(place, count), own],
                x_send.at[distance, turn - 1],
                x_recv.at[distance, turn - 1],
                here.across(turn),
            )
            for turn in range(1, peers)
        ]
    add_up(length, firsts, by_first, pool_total, pool)
    for distance in range(half_z, 0, -1):
        if distance not in steps_z.values():
            send_z(distance)
    for at in range(ring_y):
        arrived[at, own] = slots[at, own]
        choosers[at] = chooser(pick_rows[at, :1], images, length)

    def summed(place):
        return jnp.dot(choosers[place], arrived[place], preferred_element_type=jnp.float32)

    def wait_x(distance):
        for copy in x_copies[distance]:
            copy.wait_recv()

    def joined(total, ins, way, distance, half):
        if distance < half:
            return total + ins[way, distance - 1].astype(jnp.float32)
        low = way * (rows // 2)
        added = ins[way, distance - 1, low : low + rows // 2].astype(jnp.float32)
        added = added + total[low : low + rows // 2]
        rest = total[rows // 2 :] if way == 0 else total[: rows // 2]
        return jnp.concatenate([added, rest] if way == 0 else [rest, added], axis=0)

    def collect(total, way, distance, steps, copies, ins, half):
        for farther in sorted(steps, reverse=True):
            if steps[farther] == distance:
                copies[farther, way].wait_recv()
                total = joined(total, ins, way, farther, half)
        return total

    along_z = (steps_z, z_copies, z_in, half_z)
    along_y = (steps_y, y_copies, y_in, half_y)
    for distance in range(max(half_y, half_z), 0, -1):
        if distance <= half_y:
            wait_x(distance)
            for way, turn in enumerate((1, -1)):
                if distance < half_y or way == 0:
                    mine = summed(place_of(turn * distance, ring_y))
                total = collect(mine, way, distance, *along_y)
                y_out[way, distance - 1] = total.astype(jnp.bfloat16)
            send_y(distance)
        if distance <= half_z and distance in steps_z.values():
            for way, turn in enumerate((1, -1)):
                mine = pool[here.z_at(turn * distance)].astype(jnp.float32)
                total = collect(mine, way, distance, *along_z)
                z_out[way, distance - 1] = total.astype(jnp.bfloat16)
            send_z(distance)
    wait_x(0)
    gradient = summed(0) + pool[here.z].astype(jnp.float32)
    projected = feature[...]
    mean_square = jnp.mean(projected * projected, axis=-1, keepdims=True)
    inv_rms = lax.rsqrt(mean_square + EPSILON)
    normed = projected * inv_rms
    for way in range(2):
        gradient = collect(gradient, way, 0, *along_z)
        gradient = collect(gradient, way, 0, *along_y)
    mean = jnp.mean(gradient * normed, axis=-1, keepdims=True)
    feature_grad[...] = (inv_rms * (gradient - normed * mean)).astype(jnp.bfloat16)
    for copy in [*y_copies.values(), *z_copies.values(), *sum(x_copies.values(), [])]:
        copy.wait_send()


def in_vmem(count):
    return [pl.BlockSpec(memory_space=pltpu.VMEM)] * count


def in_smem(count):
    return [pl.BlockSpec(memory_space=pltpu.SMEM)] * count


def ring_semaphores(half_y, half_z, peers):
    dma = pltpu.SemaphoreType.DMA
    pairs = [(2, half_y), (2, half_z), (half_y + 1, peers - 1)]
    return [dma(shape) for shape in pairs for _ in range(2)]


def local(
    grid,
    ring_z,
    steps_y,
    steps_z,
    tokens,
    proj_weight,
    match_grad,
    edge_first,
    pair_second_image,
    send_pick,
):
    images, length, width = tokens.shape
    rows = images * length
    pairs = edge_first.shape[0]
    ring_y, peers = grid[1], grid[0] * grid[2]
    half_y, half_z = ring_y // 2, ring_z // 2
    layout = (grid, ring_z, steps_y, steps_z, images, length)
    bf16, f32 = jnp.bfloat16, jnp.float32
    shape = jax.ShapeDtypeStruct
    pool_rows, slot_rows = ring_z * rows, ring_y * peers * length

    pool, received, laid, firsts, places, pick_rows, feature = pl.pallas_call(
        functools.partial(gather_kernel, *layout),
        out_shape=(
            shape((ring_z, rows, width), bf16),
            shape((ring_y, peers * length, width), bf16),
            shape((length * spread(pairs * length // LANES), LANES), f32),
            shape((1, pairs), jnp.int32),
            shape((1, pairs), jnp.int32),
            shape((ring_y, 8, peers * length), f32),
            shape((rows, width), f32),
        ),
        in_specs=[pl.BlockSpec(memory_space=pltpu.HBM)] * 6,
        out_specs=tuple(in_vmem(7)),
        scratch_shapes=[
            pltpu.SMEM((send_pick.shape[0],), jnp.int32),
            pltpu.VMEM((rows, width), bf16),
            pltpu.VMEM(proj_weight.shape, bf16),
            pltpu.VMEM(match_grad.shape, bf16),
            pltpu.VMEM((1, pairs), jnp.int32),
            pltpu.VMEM((ring_y, rows + 16, width), bf16),
            pltpu.VMEM((ring_y, peers * length, width), bf16),
            pltpu.SemaphoreType.DMA((6,)),
            *ring_semaphores(half_y, half_z, peers),
        ],
        compiler_params=pltpu.CompilerParams(
            collective_id=0, has_side_effects=True, vmem_limit_bytes=VMEM_LIMIT
        ),
        name="gather_images",
    )(
        *(
            pltpu.with_memory_space_constraint(argument, pltpu.HBM)
            for argument in (
                send_pick,
                tokens.reshape(rows, width),
                proj_weight,
                match_grad,
                edge_first.reshape(1, pairs),
                pair_second_image.reshape(1, pairs),
            )
        )
    )

    feature_grad = pl.pallas_call(
        functools.partial(return_kernel, *layout),
        out_shape=shape((rows, width), bf16),
        in_specs=in_smem(2) + in_vmem(7),
        out_specs=pl.BlockSpec(memory_space=pltpu.VMEM),
        scratch_shapes=[
            pltpu.VMEM((width // LANES, length * spread(pairs), LANES), f32),
            pltpu.VMEM((width // LANES, length * spread(pairs), LANES), f32),
            pltpu.VMEM((width // LANES, pool_rows // length * spread(length), LANES), f32),
            pltpu.VMEM((width // LANES, slot_rows // length * spread(length), LANES), f32),
            pltpu.VMEM((ring_y, peers * length, width), bf16),
            pltpu.VMEM((ring_z, rows, width), bf16),
            pltpu.VMEM((ring_y, peers * length, width), bf16),
            pltpu.VMEM((ring_y, rows, peers * length), bf16),
            pltpu.VMEM((2, half_y, rows, width), bf16),
            pltpu.VMEM((2, half_y, rows, width), bf16),
            pltpu.VMEM((2, half_z, rows, width), bf16),
            pltpu.VMEM((2, half_z, rows, width), bf16),
            *ring_semaphores(half_y, half_z, peers),
        ],
        compiler_params=pltpu.CompilerParams(
            collective_id=1, has_side_effects=True, vmem_limit_bytes=VMEM_LIMIT
        ),
        name="return_gradients",
    )(
        firsts,
        places,
        firsts,
        places,
        pool.reshape(pool_rows // length, length, width),
        received.reshape(slot_rows // length, length, width),
        laid,
        pick_rows,
        feature,
    )
    token_grad = lax.dot_general(
        feature_grad, proj_weight, (((1,), (1,)), ((), ())), preferred_element_type=f32
    )
    return token_grad.astype(bf16).reshape(images, length, width)


def solution(mesh, grid=GRID, steps_y=STEPS_Y, steps_z=STEPS_Z):
    placed = (
        P(("grp", "sub"), None, None),
        P(),
        P(("grp", "sub"), None),
        P(("grp", "sub")),
        P(("grp", "sub")),
        P(("grp", "sub")),
    )
    return jax.shard_map(
        functools.partial(local, grid, mesh.shape["sub"], steps_y, steps_z),
        mesh=mesh,
        in_specs=placed,
        out_specs=P(("grp", "sub"), None, None),
        check_vma=False,
    )
```

```python
import functools

import jax
import jax.numpy as jnp
from jax import lax
from jax.experimental import pallas as pl
from jax.experimental.pallas import tpu as pltpu
from jax.sharding import PartitionSpec as P

EPSILON = 1e-05
SOFTMAX_COOLING = 0.1
MESH = pl.DeviceIdType.MESH
LANES = 128
VMEM_LIMIT = 40 * 1024 * 1024
GRID = (4, 8, 2)
STEPS_Y = {1: 0, 2: 0, 3: 1, 4: 2}
STEPS_Z = {2: 0, 1: 0, 4: 2, 3: 2, 6: 4, 5: 4}
ARRIVALS = (
    ("y", 1),
    ("z", 2),
    ("y", 2),
    ("z", 1),
    ("z", 4),
    ("y", 3),
    ("y", 4),
    ("z", 3),
    ("z", 6),
    ("z", 5),
)


def place_of(offset, ring):
    offset %= ring
    return 0 if offset == 0 else 2 * offset - 1 if 2 * offset <= ring else 2 * (ring - offset)


class Where:
    def __init__(self, grid, ring_z):
        _, self.ring_y, cores = grid
        self.cores, self.ring_z, self.peers = cores, ring_z, grid[0] * cores
        grp = lax.axis_index("grp")
        self.z = lax.axis_index("sub")
        self.y = lax.rem(lax.div(grp, cores), self.ring_y)
        self.s = lax.div(grp, cores * self.ring_y) * cores + lax.rem(grp, cores)

    def group(self, s, y):
        return (lax.div(s, self.cores) * self.ring_y + y) * self.cores + lax.rem(s, self.cores)

    def along_y(self, step):
        return {"grp": self.group(self.s, lax.rem(self.y + step + self.ring_y, self.ring_y))}

    def z_at(self, step):
        return lax.rem(self.z + step + self.ring_z, self.ring_z)

    def along_z(self, step):
        return {"sub": self.z_at(step)}

    def s_at(self, turn):
        return lax.rem(self.s + turn, self.peers)

    def across(self, turn):
        return {"grp": self.group(self.s_at(turn), self.y)}

    def greet(self, steps_y, steps_z):
        barrier = pltpu.get_barrier_semaphore()
        others = []
        for hop in sorted({distance - before for distance, before in steps_y.items()}):
            others += [self.along_y(hop), self.along_y(-hop)]
        for hop in sorted({distance - before for distance, before in steps_z.items()}):
            others += [self.along_z(hop), self.along_z(-hop)]
        others += [self.across(turn) for turn in range(1, self.peers)]
        for other in others:
            pl.semaphore_signal(barrier, inc=1, device_id=other, device_id_type=MESH)
        return lambda: pl.semaphore_wait(barrier, len(others))


def send(src, dst, send_sem, recv_sem, device):
    copy = pltpu.make_async_remote_copy(
        src_ref=src,
        dst_ref=dst,
        send_sem=send_sem,
        recv_sem=recv_sem,
        device_id=device,
        device_id_type=MESH,
    )
    copy.start()
    return copy


def batches(ring):
    half = ring // 2
    return [(0, 1)] + [(2 * d - 1, 2) for d in range(1, half)] + [(ring - 1, 1)]


def spread(count):
    return (count // 8 | 1) * 8


def rows_at(index, count):
    return pl.ds(pl.multiple_of(index * count, count), count)


def chooser(pick_row, images, length):
    shape = (images * length, pick_row.shape[1])
    row = lax.broadcasted_iota(jnp.int32, shape, 0)
    column = lax.broadcasted_iota(jnp.int32, shape, 1)
    image = lax.div(row, length).astype(jnp.float32)
    same = lax.rem(row, length) == lax.rem(column, length)
    return jnp.where(same & (image == pick_row), 1.0, 0.0).astype(jnp.bfloat16)


def gather(
    here,
    steps_y,
    steps_z,
    images,
    length,
    arguments,
    pool,
    received,
    laid,
    first_ref,
    firsts,
    place_ref,
    places,
    pick_rows,
    feature,
    picks,
    second_ref,
    tokens,
    weight,
    grads,
    seconds,
    blocks,
    stage,
    fetch_sem,
    y_send,
    y_recv,
    z_send,
    z_recv,
    x_send,
    x_recv,
):
    ring_y, ring_z, peers = here.ring_y, here.ring_z, here.peers
    rows, width = tokens.shape
    block_rows = blocks.shape[1]
    picks_arg, tokens_arg, weight_arg, grads_arg, firsts_arg, seconds_arg = arguments
    fetches = [
        pltpu.make_async_copy(src, dst, fetch_sem.at[n])
        for n, (src, dst) in enumerate(
            (
                (tokens_arg, tokens),
                (weight_arg, weight),
                (picks_arg, picks),
                (seconds_arg, seconds),
                (seconds_arg, second_ref),
                (firsts_arg, firsts),
                (firsts_arg, first_ref),
                (grads_arg, grads),
            )
        )
    ]
    for fetch in fetches:
        fetch.start()
    met = here.greet(steps_y, steps_z)

    for fetch in fetches[:3]:
        fetch.wait()
    projected = jnp.dot(tokens[...], weight[...], preferred_element_type=jnp.float32)
    feature[...] = projected
    mean_square = jnp.mean(projected * projected, axis=-1, keepdims=True)
    normed = (projected * lax.rsqrt(mean_square + EPSILON)).astype(jnp.bfloat16)
    blocks[0, :rows] = normed
    for n in range(images):
        pool[here.z * images + n] = normed[n * length : (n + 1) * length]
    tail = (block_rows - rows, peers * length)
    tail_row = lax.broadcasted_iota(jnp.int32, tail, 0)
    tail_peer = lax.div(lax.broadcasted_iota(jnp.int32, tail, 1), length)
    table = jnp.zeros(tail, jnp.int32)
    for y in range(ring_y):
        for s in range(peers):
            slot = (s // here.cores * ring_y + y) * here.cores + s % here.cores
            table = jnp.where((tail_row == y) & (tail_peer == s), picks[slot], table)
    blocks[0, rows:] = table.astype(jnp.float32).astype(jnp.bfloat16)
    met()

    half_y, half_z = ring_y // 2, ring_z // 2
    y_copies, z_copies, x_copies = {}, {}, []

    def forward_y(source):
        for distance, before in steps_y.items():
            if before != source:
                continue
            for way, turn in enumerate((1, -1)):
                part = pl.ds(0, block_rows)
                if distance == half_y:
                    part = pl.ds(0, rows // 2) if way == 0 else pl.ds(rows // 2, block_rows - rows // 2)
                y_copies[distance, way] = send(
                    blocks.at[place_of(-turn * before, ring_y), part],
                    blocks.at[place_of(-turn * distance, ring_y), part],
                    y_send.at[way, distance - 1],
                    y_recv.at[way, distance - 1],
                    here.along_y(turn * (distance - before)),
                )

    def forward_z(source):
        for distance, before in steps_z.items():
            if before != source:
                continue
            for way, turn in enumerate((1, -1)):
                first = here.z_at(-turn * before) * images
                part = pl.ds(first, images)
                if distance == half_z:
                    part = pl.ds(first + way * (images // 2), images // 2)
                z_copies[distance, way] = send(
                    pool.at[part],
                    pool.at[part],
                    z_send.at[way, distance - 1],
                    z_recv.at[way, distance - 1],
                    here.along_z(turn * (distance - before)),
                )

    own = rows_at(here.s, length)

    def choose(batch, place, count):
        for at in range(place, place + count):
            rows_of_y = blocks[at, rows:].astype(jnp.float32)
            mine = jnp.sum(jnp.where(tail_row == here.y, rows_of_y, 0.0), axis=0, keepdims=True)
            pick_rows[at] = jnp.broadcast_to(mine, pick_rows.shape[1:])
            stage[at] = lax.dot_general(
                chooser(mine, images, length),
                blocks[at, :rows],
                (((0,), (0,)), ((), ())),
                preferred_element_type=jnp.float32,
            ).astype(jnp.bfloat16)
        for turn in range(1, peers):
            x_copies.append(
                send(
                    stage.at[pl.ds(place, count), rows_at(here.s_at(turn), length)],
                    received.at[pl.ds(place, count), here.s],
                    x_send.at[batch, turn - 1],
                    x_recv.at[batch, turn - 1],
                    here.across(turn),
                )
            )
        for at in range(place, place + count):
            received[at, here.s] = stage[at, own]

    forward_y(0)
    forward_z(0)
    plan = batches(ring_y)
    choose(0, *plan[0])
    for fetch in fetches[3:]:
        fetch.wait()

    def find(slot):
        offset = lax.rem(lax.rem(lax.div(slot, here.cores), ring_y) - here.y + ring_y, ring_y)
        near = jnp.where(2 * offset <= ring_y, 2 * offset - 1, 2 * (ring_y - offset))
        peer = lax.div(slot, here.cores * ring_y) * here.cores + lax.rem(slot, here.cores)
        return jnp.where(offset == 0, 0, near), peer

    place, peer = find(seconds[...])
    places[...] = place * peers + peer

    def note(e, carry):
        place_ref[0, e], place_ref[1, e] = find(second_ref[0, e])
        return carry

    lax.fori_loop(0, second_ref.shape[1], note, 0)

    across = LANES // length
    groups = grads.shape[0] // across
    lane_block = lax.div(lax.broadcasted_iota(jnp.int32, (groups, LANES), 1), length)

    def lay(tile):
        wide = grads[:, tile * LANES : (tile + 1) * LANES].astype(jnp.float32)
        parts = [wide[q * groups : (q + 1) * groups] for q in range(across)]
        for r in range(across):
            total = None
            for q in range(across):
                shift = (q - r) % across * length
                moved = pltpu.roll(parts[q], shift, 1) if shift else parts[q]
                total = moved if total is None else jnp.where(lane_block == q, moved, total)
            i = tile * across + r
            laid[i * spread(groups) : i * spread(groups) + groups] = total

    tiles = grads.shape[1] // LANES
    todo = list(range(tiles))
    for axis, distance in ARRIVALS:
        if todo:
            lay(todo.pop(0))
        if axis == "y" and distance <= half_y:
            for way in range(2):
                y_copies[distance, way].wait_recv()
            forward_y(distance)
            choose(distance, *plan[distance])
        if axis == "z" and distance <= half_z:
            for way in range(2):
                z_copies[distance, way].wait_recv()
            forward_z(distance)
    for tile in todo:
        lay(tile)
    for copy in x_copies:
        copy.wait_recv()
    for copy in [*y_copies.values(), *z_copies.values(), *x_copies]:
        copy.wait_send()


def pair_gradients(length, first_ref, place_ref, pool, received, laid, by_first, by_second):
    pairs = first_ref.shape[1]
    across = LANES // length
    groups = pairs // across
    width = pool.shape[2]
    scale = 1.0 / (width * SOFTMAX_COOLING)
    together = groups

    side = (LANES, LANES)
    row_block = lax.div(lax.broadcasted_iota(jnp.int32, side, 0), length)
    lane_block = lax.div(lax.broadcasted_iota(jnp.int32, side, 1), length)
    diagonal = row_block == lane_block
    ones = jnp.where(diagonal, 1.0, 0.0).astype(jnp.bfloat16)
    ones = jnp.concatenate([ones, ones], axis=0)
    narrow = lax.div(lax.broadcasted_iota(jnp.int32, (length, LANES), 1), length)

    def block_sums(values):
        high = values.astype(jnp.bfloat16)
        low = (values - high.astype(jnp.float32)).astype(jnp.bfloat16)
        return jnp.dot(
            jnp.concatenate([high, low], axis=1), ones, preferred_element_type=jnp.float32
        )

    def step(chunk, carry):
        firsts, seconds, scores, incoming = [], [], [], []
        for n in range(together):
            g = chunk * together + n
            pairs_of_g = [q * groups + g for q in range(across)]
            firsts.append(jnp.concatenate([pool[first_ref[0, e]] for e in pairs_of_g], axis=0))
            seconds.append(
                jnp.concatenate(
                    [received[place_ref[0, e], place_ref[1, e]] for e in pairs_of_g], axis=0
                )
            )
            full = lax.dot_general(
                firsts[n],
                seconds[n],
                (((1,), (1,)), ((), ())),
                preferred_element_type=jnp.float32,
            )
            packed = full[:length]
            for q in range(1, across):
                packed = jnp.where(narrow == q, full[q * length : (q + 1) * length], packed)
            scores.append(packed)
            incoming.append(laid[pl.ds(g, length, stride=spread(groups)), :])
        shape = (together, length, LANES)
        expo = jnp.exp(jnp.concatenate(scores, axis=0) * scale)
        gradient = jnp.concatenate(incoming, axis=0)
        rows = expo / block_sums(expo)
        expo = expo.reshape(shape)
        cols = (expo / jnp.sum(expo, axis=1, keepdims=True)).reshape(rows.shape)
        both = gradient * rows * cols
        over_second = block_sums(both)
        over_first = jnp.sum(both.reshape(shape), axis=1, keepdims=True)
        part = (cols.reshape(shape) * over_first).reshape(rows.shape)
        d_scaled = ((2.0 * both - rows * over_second - part) * scale).astype(jnp.bfloat16)
        for n in range(together):
            mine = d_scaled[n * length : (n + 1) * length]
            wide = jnp.concatenate([mine] * across, axis=0)
            wide = jnp.where(diagonal, wide, jnp.zeros_like(wide))
            grad_first = jnp.dot(wide, seconds[n], preferred_element_type=jnp.float32)
            grad_second = lax.dot_general(
                wide, firsts[n], (((0,), (0,)), ((), ())), preferred_element_type=jnp.float32
            )
            for q in range(across):
                part = slice(q * length, (q + 1) * length)
                rows_of_pair = pl.ds(q * groups + chunk * together + n, length, stride=spread(pairs))
                for h in range(width // LANES):
                    lanes = slice(h * LANES, (h + 1) * LANES)
                    by_first[h, rows_of_pair, :] = grad_first[part, lanes]
                    by_second[h, rows_of_pair, :] = grad_second[part, lanes]
        return carry

    lax.fori_loop(0, groups // together, step, 0)


def add_up(length, image_of_pair, by_pair, total, rounded):
    pairs = image_of_pair.shape[1]
    far = spread(length)
    halves, count = total.shape[0], total.shape[1] // far
    image = lax.broadcasted_iota(jnp.int32, (count, pairs), 0)
    chosen = jnp.where(image == image_of_pair[...], 1.0, 0.0).astype(jnp.bfloat16)
    together = length

    def step(chunk, carry):
        for n in range(together):
            i = chunk * together + n
            rows_of_i = pl.ds(pl.multiple_of(i * spread(pairs), 8), pairs)
            rows_of_i = [by_pair[h, rows_of_i].astype(jnp.bfloat16) for h in range(halves)]
            sums = jnp.dot(
                chosen, jnp.concatenate(rows_of_i, axis=1), preferred_element_type=jnp.float32
            )
            for h in range(halves):
                lanes = slice(h * LANES, (h + 1) * LANES)
                total[h, pl.ds(i, count, stride=far), :] = sums[:, lanes]
        return carry

    lax.fori_loop(0, length // together, step, 0)
    images = rounded.shape[1] // length
    for n in range(count):
        rows_of_image = slice(n % images * length, (n % images + 1) * length)
        for h in range(halves):
            rounded[n // images, rows_of_image, h * LANES : (h + 1) * LANES] = total[
                h, n * far : n * far + length
            ].astype(jnp.bfloat16)


def give_back(
    here,
    steps_y,
    steps_z,
    images,
    length,
    sum_pool,
    slots,
    pool,
    pick_rows,
    feature,
    arrived,
    choosers,
    y_in,
    y_out,
    z_in,
    z_out,
    y_send,
    y_recv,
    z_send,
    z_recv,
    x_send,
    x_recv,
):
    ring_y, ring_z, peers = here.ring_y, here.ring_z, here.peers
    rows, width = feature.shape
    half_y, half_z = ring_y // 2, ring_z // 2
    own = rows_at(here.s, length)
    plan = batches(ring_y)
    y_copies, z_copies, x_copies = {}, {}, {}

    def part_of(distance, way, half):
        return pl.ds(way * (rows // 2), rows // 2) if distance == half else pl.ds(0, rows)

    def send_z(distance):
        hop = distance - steps_z[distance]
        for way, turn in enumerate((1, -1)):
            part = part_of(distance, way, half_z)
            if distance in steps_z.values():
                source = z_out.at[way, distance - 1, part]
            else:
                source = pool.at[here.z_at(turn * distance), part]
            z_copies[distance, way] = send(
                source,
                z_in.at[way, distance - 1, part],
                z_send.at[way, distance - 1],
                z_recv.at[way, distance - 1],
                here.along_z(turn * hop),
            )

    def send_y(distance):
        hop = distance - steps_y[distance]
        for way, turn in enumerate((1, -1)):
            part = part_of(distance, way, half_y)
            y_copies[distance, way] = send(
                y_out.at[way, distance - 1, part],
                y_in.at[way, distance - 1, part],
                y_send.at[way, distance - 1],
                y_recv.at[way, distance - 1],
                here.along_y(turn * hop),
            )

    for distance in range(half_y, -1, -1):
        place, count = plan[distance]
        x_copies[distance] = [
            send(
                slots.at[pl.ds(place, count), rows_at(here.s_at(turn), length)],
                arrived.at[pl.ds(place, count), own],
                x_send.at[distance, turn - 1],
                x_recv.at[distance, turn - 1],
                here.across(turn),
            )
            for turn in range(1, peers)
        ]
    sum_pool()
    for distance in range(half_z, 0, -1):
        if distance not in steps_z.values():
            send_z(distance)
    for at in range(ring_y):
        arrived[at, own] = slots[at, own]
        choosers[at] = chooser(pick_rows[at, :1], images, length)

    def summed(place):
        return jnp.dot(choosers[place], arrived[place], preferred_element_type=jnp.float32)

    def wait_x(distance):
        for copy in x_copies[distance]:
            copy.wait_recv()

    def joined(total, ins, way, distance, half):
        if distance < half:
            return total + ins[way, distance - 1].astype(jnp.float32)
        low = way * (rows // 2)
        added = ins[way, distance - 1, low : low + rows // 2].astype(jnp.float32)
        added = added + total[low : low + rows // 2]
        rest = total[rows // 2 :] if way == 0 else total[: rows // 2]
        return jnp.concatenate([added, rest] if way == 0 else [rest, added], axis=0)

    def collect(total, way, distance, steps, copies, ins, half):
        for farther in sorted(steps, reverse=True):
            if steps[farther] == distance:
                copies[farther, way].wait_recv()
                total = joined(total, ins, way, farther, half)
        return total

    along_z = (steps_z, z_copies, z_in, half_z)
    along_y = (steps_y, y_copies, y_in, half_y)
    for distance in range(max(half_y, half_z), 0, -1):
        if distance <= half_y:
            wait_x(distance)
            for way, turn in enumerate((1, -1)):
                if distance < half_y or way == 0:
                    mine = summed(place_of(turn * distance, ring_y))
                total = collect(mine, way, distance, *along_y)
                y_out[way, distance - 1] = total.astype(jnp.bfloat16)
            send_y(distance)
        if distance <= half_z and distance in steps_z.values():
            for way, turn in enumerate((1, -1)):
                mine = pool[here.z_at(turn * distance)].astype(jnp.float32)
                total = collect(mine, way, distance, *along_z)
                z_out[way, distance - 1] = total.astype(jnp.bfloat16)
            send_z(distance)
    wait_x(0)
    gradient = summed(0) + pool[here.z].astype(jnp.float32)
    projected = feature[...]
    mean_square = jnp.mean(projected * projected, axis=-1, keepdims=True)
    inv_rms = lax.rsqrt(mean_square + EPSILON)
    normed = projected * inv_rms
    for way in range(2):
        gradient = collect(gradient, way, 0, *along_z)
        gradient = collect(gradient, way, 0, *along_y)
    mean = jnp.mean(gradient * normed, axis=-1, keepdims=True)
    for copy in [*y_copies.values(), *z_copies.values(), *sum(x_copies.values(), [])]:
        copy.wait_send()
    return (inv_rms * (gradient - normed * mean)).astype(jnp.bfloat16)


def kernel(grid, ring_z, steps_y, steps_z, images, length, *refs):
    arguments, (feature_grad, *scratch) = refs[:6], refs[6:]
    gathered, fetched, moved, sems = scratch[:9], scratch[9:17], scratch[17:29], scratch[29:]
    pool_images, received, laid, first_ref, firsts, place_ref, places, pick_rows, feature = gathered
    by_first, by_second, pool_total, slot_total, slots, pool, *rings = moved
    here = Where(grid, ring_z)
    common = (here, steps_y, steps_z, images, length)
    gather(*common, arguments, *gathered, *fetched, *sems[:7])
    pair_gradients(length, first_ref, place_ref, pool_images, received, laid, by_first, by_second)
    add_up(length, places, by_second, slot_total, slots)
    feature_grad[...] = give_back(
        *common,
        lambda: add_up(length, firsts, by_first, pool_total, pool),
        slots,
        pool,
        pick_rows,
        feature,
        *rings,
        *sems[7:],
    )


def ring_semaphores(half_y, half_z, peers):
    dma = pltpu.SemaphoreType.DMA
    pairs = [(2, half_y), (2, half_z), (half_y + 1, peers - 1)]
    return [dma(shape) for shape in pairs for _ in range(2)]


def local(
    grid,
    ring_z,
    steps_y,
    steps_z,
    tokens,
    proj_weight,
    match_grad,
    edge_first,
    pair_second_image,
    send_pick,
):
    images, length, width = tokens.shape
    rows = images * length
    pairs = edge_first.shape[0]
    ring_y, peers = grid[1], grid[0] * grid[2]
    half_y, half_z = ring_y // 2, ring_z // 2
    layout = (grid, ring_z, steps_y, steps_z, images, length)
    bf16, f32 = jnp.bfloat16, jnp.float32

    block = (ring_y, peers * length, width)
    feature_grad = pl.pallas_call(
        functools.partial(kernel, *layout),
        out_shape=jax.ShapeDtypeStruct((rows, width), bf16),
        in_specs=[pl.BlockSpec(memory_space=pltpu.HBM)] * 6,
        out_specs=pl.BlockSpec(memory_space=pltpu.VMEM),
        scratch_shapes=[
            pltpu.VMEM((ring_z * images, length, width), bf16),
            pltpu.VMEM((ring_y, peers, length, width), bf16),
            pltpu.VMEM((length * spread(pairs * length // LANES), LANES), f32),
            pltpu.SMEM((1, pairs), jnp.int32),
            pltpu.VMEM((1, pairs), jnp.int32),
            pltpu.SMEM((2, pairs), jnp.int32),
            pltpu.VMEM((1, pairs), jnp.int32),
            pltpu.VMEM((ring_y, 8, peers * length), f32),
            pltpu.VMEM((rows, width), f32),
            pltpu.SMEM((send_pick.shape[0],), jnp.int32),
            pltpu.SMEM((1, pairs), jnp.int32),
            pltpu.VMEM((rows, width), bf16),
            pltpu.VMEM(proj_weight.shape, bf16),
            pltpu.VMEM(match_grad.shape, bf16),
            pltpu.VMEM((1, pairs), jnp.int32),
            pltpu.VMEM((ring_y, rows + 16, width), bf16),
            pltpu.VMEM(block, bf16),
            pltpu.VMEM((width // LANES, length * spread(pairs), LANES), f32),
            pltpu.VMEM((width // LANES, length * spread(pairs), LANES), f32),
            pltpu.VMEM((width // LANES, ring_z * images * spread(length), LANES), f32),
            pltpu.VMEM((width // LANES, ring_y * peers * spread(length), LANES), f32),
            pltpu.VMEM(block, bf16),
            pltpu.VMEM((ring_z, rows, width), bf16),
            pltpu.VMEM(block, bf16),
            pltpu.VMEM((ring_y, rows, peers * length), bf16),
            pltpu.VMEM((2, half_y, rows, width), bf16),
            pltpu.VMEM((2, half_y, rows, width), bf16),
            pltpu.VMEM((2, half_z, rows, width), bf16),
            pltpu.VMEM((2, half_z, rows, width), bf16),
            pltpu.SemaphoreType.DMA((8,)),
            *ring_semaphores(half_y, half_z, peers),
            *ring_semaphores(half_y, half_z, peers),
        ],
        compiler_params=pltpu.CompilerParams(
            collective_id=0, has_side_effects=True, vmem_limit_bytes=VMEM_LIMIT
        ),
        name="feature_gradients",
    )(
        *(
            pltpu.with_memory_space_constraint(argument, pltpu.HBM)
            for argument in (
                send_pick,
                tokens.reshape(rows, width),
                proj_weight,
                match_grad,
                edge_first.reshape(1, pairs),
                pair_second_image.reshape(1, pairs),
            )
        )
    )
    token_grad = lax.dot_general(
        feature_grad, proj_weight, (((1,), (1,)), ((), ())), preferred_element_type=f32
    )
    return token_grad.astype(bf16).reshape(images, length, width)


def solution(mesh, grid=GRID, steps_y=STEPS_Y, steps_z=STEPS_Z):
    placed = (
        P(("grp", "sub"), None, None),
        P(),
        P(("grp", "sub"), None),
        P(("grp", "sub")),
        P(("grp", "sub")),
        P(("grp", "sub")),
    )
    return jax.shard_map(
        functools.partial(local, grid, mesh.shape["sub"], steps_y, steps_z),
        mesh=mesh,
        in_specs=placed,
        out_specs=P(("grp", "sub"), None, None),
        check_vma=False,
    )
```

```python
import functools

import jax
import jax.numpy as jnp
from jax import lax
from jax.experimental import pallas as pl
from jax.experimental.pallas import tpu as pltpu
from jax.sharding import PartitionSpec as P

EPSILON = 1e-05
SOFTMAX_COOLING = 0.1
MESH = pl.DeviceIdType.MESH
LANES = 128
VMEM_LIMIT = 40 * 1024 * 1024
GRID = (4, 8, 2)
STEPS_Y = {1: 0, 2: 0, 3: 1, 4: 2}
STEPS_Z = {2: 0, 1: 0, 4: 2, 3: 2, 6: 4, 5: 4}
ARRIVALS = (
    ("y", 1),
    ("z", 2),
    ("y", 2),
    ("z", 1),
    ("z", 4),
    ("y", 3),
    ("y", 4),
    ("z", 3),
    ("z", 6),
    ("z", 5),
)


def place_of(offset, ring):
    offset %= ring
    return 0 if offset == 0 else 2 * offset - 1 if 2 * offset <= ring else 2 * (ring - offset)


class Where:
    def __init__(self, grid, ring_z):
        _, self.ring_y, cores = grid
        self.cores, self.ring_z, self.peers = cores, ring_z, grid[0] * cores
        grp = lax.axis_index("grp")
        self.z = lax.axis_index("sub")
        self.y = lax.rem(lax.div(grp, cores), self.ring_y)
        self.s = lax.div(grp, cores * self.ring_y) * cores + lax.rem(grp, cores)

    def group(self, s, y):
        return (lax.div(s, self.cores) * self.ring_y + y) * self.cores + lax.rem(s, self.cores)

    def along_y(self, step):
        return {"grp": self.group(self.s, lax.rem(self.y + step + self.ring_y, self.ring_y))}

    def z_at(self, step):
        return lax.rem(self.z + step + self.ring_z, self.ring_z)

    def along_z(self, step):
        return {"sub": self.z_at(step)}

    def s_at(self, turn):
        return lax.rem(self.s + turn, self.peers)

    def across(self, turn):
        return {"grp": self.group(self.s_at(turn), self.y)}

    def greet(self, steps_y, steps_z):
        barrier = pltpu.get_barrier_semaphore()
        others = []
        for hop in sorted({distance - before for distance, before in steps_y.items()}):
            others += [self.along_y(hop), self.along_y(-hop)]
        for hop in sorted({distance - before for distance, before in steps_z.items()}):
            others += [self.along_z(hop), self.along_z(-hop)]
        others += [self.across(turn) for turn in range(1, self.peers)]
        for other in others:
            pl.semaphore_signal(barrier, inc=1, device_id=other, device_id_type=MESH)
        return lambda: pl.semaphore_wait(barrier, len(others))


def send(src, dst, send_sem, recv_sem, device):
    copy = pltpu.make_async_remote_copy(
        src_ref=src,
        dst_ref=dst,
        send_sem=send_sem,
        recv_sem=recv_sem,
        device_id=device,
        device_id_type=MESH,
    )
    copy.start()
    return copy


def batches(ring):
    half = ring // 2
    return [(0, 1)] + [(2 * d - 1, 2) for d in range(1, half)] + [(ring - 1, 1)]


def spread(count):
    return (count // 8 | 1) * 8


def rows_at(index, count):
    return pl.ds(pl.multiple_of(index * count, count), count)


def chooser(pick_row, images, length):
    shape = (images * length, pick_row.shape[1])
    row = lax.broadcasted_iota(jnp.int32, shape, 0)
    column = lax.broadcasted_iota(jnp.int32, shape, 1)
    image = lax.div(row, length).astype(jnp.float32)
    same = lax.rem(row, length) == lax.rem(column, length)
    return jnp.where(same & (image == pick_row), 1.0, 0.0).astype(jnp.bfloat16)


def gather(
    here,
    steps_y,
    steps_z,
    images,
    length,
    arguments,
    pool,
    received,
    laid,
    first_ref,
    firsts,
    place_ref,
    places,
    pick_rows,
    feature,
    picks,
    second_ref,
    tokens,
    weight,
    grads,
    seconds,
    blocks,
    stage,
    fetch_sem,
    y_send,
    y_recv,
    z_send,
    z_recv,
    x_send,
    x_recv,
):
    ring_y, ring_z, peers = here.ring_y, here.ring_z, here.peers
    rows, width = tokens.shape
    block_rows = blocks.shape[1]
    picks_arg, tokens_arg, weight_arg, grads_arg, firsts_arg, seconds_arg = arguments
    met = here.greet(steps_y, steps_z)
    fetches = [
        pltpu.make_async_copy(src, dst, fetch_sem.at[n])
        for n, (src, dst) in enumerate(
            (
                (tokens_arg, tokens),
                (weight_arg, weight),
                (picks_arg, picks),
                (seconds_arg, seconds),
                (seconds_arg, second_ref),
                (firsts_arg, firsts),
                (firsts_arg, first_ref),
                (grads_arg, grads),
            )
        )
    ]
    for fetch in fetches:
        fetch.start()
    for fetch in fetches[:3]:
        fetch.wait()
    projected = jnp.dot(tokens[...], weight[...], preferred_element_type=jnp.float32)
    feature[...] = projected
    mean_square = jnp.mean(projected * projected, axis=-1, keepdims=True)
    normed = (projected * lax.rsqrt(mean_square + EPSILON)).astype(jnp.bfloat16)
    blocks[0, :rows] = normed
    for n in range(images):
        pool[here.z * images + n] = normed[n * length : (n + 1) * length]
    tail = (block_rows - rows, peers * length)
    tail_row = lax.broadcasted_iota(jnp.int32, tail, 0)
    tail_peer = lax.div(lax.broadcasted_iota(jnp.int32, tail, 1), length)
    table = jnp.zeros(tail, jnp.int32)
    for y in range(ring_y):
        for s in range(peers):
            slot = (s // here.cores * ring_y + y) * here.cores + s % here.cores
            table = jnp.where((tail_row == y) & (tail_peer == s), picks[slot], table)
    blocks[0, rows:] = table.astype(jnp.float32).astype(jnp.bfloat16)
    met()

    half_y, half_z = ring_y // 2, ring_z // 2
    y_copies, z_copies, x_copies = {}, {}, []

    def forward_y(source):
        for distance, before in steps_y.items():
            if before != source:
                continue
            for way, turn in enumerate((1, -1)):
                part = pl.ds(0, block_rows)
                if distance == half_y:
                    part = pl.ds(0, rows // 2) if way == 0 else pl.ds(rows // 2, block_rows - rows // 2)
                y_copies[distance, way] = send(
                    blocks.at[place_of(-turn * before, ring_y), part],
                    blocks.at[place_of(-turn * distance, ring_y), part],
                    y_send.at[way, distance - 1],
                    y_recv.at[way, distance - 1],
                    here.along_y(turn * (distance - before)),
                )

    def forward_z(source):
        for distance, before in steps_z.items():
            if before != source:
                continue
            for way, turn in enumerate((1, -1)):
                first = here.z_at(-turn * before) * images
                part = pl.ds(first, images)
                if distance == half_z:
                    part = pl.ds(first + way * (images // 2), images // 2)
                z_copies[distance, way] = send(
                    pool.at[part],
                    pool.at[part],
                    z_send.at[way, distance - 1],
                    z_recv.at[way, distance - 1],
                    here.along_z(turn * (distance - before)),
                )

    own = rows_at(here.s, length)

    def choose(batch, place, count):
        for at in range(place, place + count):
            rows_of_y = blocks[at, rows:].astype(jnp.float32)
            mine = jnp.sum(jnp.where(tail_row == here.y, rows_of_y, 0.0), axis=0, keepdims=True)
            pick_rows[at] = jnp.broadcast_to(mine, pick_rows.shape[1:])
            stage[at] = lax.dot_general(
                chooser(mine, images, length),
                blocks[at, :rows],
                (((0,), (0,)), ((), ())),
                preferred_element_type=jnp.float32,
            ).astype(jnp.bfloat16)
        for turn in range(1, peers):
            x_copies.append(
                send(
                    stage.at[pl.ds(place, count), rows_at(here.s_at(turn), length)],
                    received.at[pl.ds(place, count), here.s],
                    x_send.at[batch, turn - 1],
                    x_recv.at[batch, turn - 1],
                    here.across(turn),
                )
            )
        for at in range(place, place + count):
            received[at, here.s] = stage[at, own]

    forward_y(0)
    forward_z(0)
    plan = batches(ring_y)
    choose(0, *plan[0])
    for fetch in fetches[3:]:
        fetch.wait()

    def find(slot):
        offset = lax.rem(lax.rem(lax.div(slot, here.cores), ring_y) - here.y + ring_y, ring_y)
        near = jnp.where(2 * offset <= ring_y, 2 * offset - 1, 2 * (ring_y - offset))
        peer = lax.div(slot, here.cores * ring_y) * here.cores + lax.rem(slot, here.cores)
        return jnp.where(offset == 0, 0, near), peer

    place, peer = find(seconds[...])
    places[...] = place * peers + peer

    def note(e, carry):
        place_ref[0, e], place_ref[1, e] = find(second_ref[0, e])
        return carry

    lax.fori_loop(0, second_ref.shape[1], note, 0)

    across = LANES // length
    groups = grads.shape[0] // across
    lane_block = lax.div(lax.broadcasted_iota(jnp.int32, (groups, LANES), 1), length)

    def lay(tile):
        wide = grads[:, tile * LANES : (tile + 1) * LANES].astype(jnp.float32)
        parts = [wide[q * groups : (q + 1) * groups] for q in range(across)]
        for r in range(across):
            total = None
            for q in range(across):
                shift = (q - r) % across * length
                moved = pltpu.roll(parts[q], shift, 1) if shift else parts[q]
                total = moved if total is None else jnp.where(lane_block == q, moved, total)
            i = tile * across + r
            laid[i * spread(groups) : i * spread(groups) + groups] = total

    tiles = grads.shape[1] // LANES
    todo = list(range(tiles))
    for axis, distance in ARRIVALS:
        if todo:
            lay(todo.pop(0))
        if axis == "y" and distance <= half_y:
            for way in range(2):
                y_copies[distance, way].wait_recv()
            forward_y(distance)
            choose(distance, *plan[distance])
        if axis == "z" and distance <= half_z:
            for way in range(2):
                z_copies[distance, way].wait_recv()
            forward_z(distance)
    for tile in todo:
        lay(tile)
    for copy in x_copies:
        copy.wait_recv()
    for copy in [*y_copies.values(), *z_copies.values(), *x_copies]:
        copy.wait_send()


def put_rows(by_pair, pair, length, pairs, values):
    for h in range(by_pair.shape[0]):
        by_pair[h, pl.ds(pair, length, stride=spread(pairs)), :] = values[
            :, h * LANES : (h + 1) * LANES
        ]


def on_diagonal(packed, length):
    side = (LANES, LANES)
    row_block = lax.div(lax.broadcasted_iota(jnp.int32, side, 0), length)
    lane_block = lax.div(lax.broadcasted_iota(jnp.int32, side, 1), length)
    wide = jnp.concatenate([packed] * (LANES // length), axis=0)
    return jnp.where(row_block == lane_block, wide, jnp.zeros_like(wide))


def first_gradients(length, place_ref, received, d_scores, by_first):
    pairs = place_ref.shape[1]
    across = LANES // length
    groups = pairs // across
    for g in range(groups):
        pairs_of_g = [q * groups + g for q in range(across)]
        second = jnp.concatenate(
            [received[place_ref[0, e], place_ref[1, e]] for e in pairs_of_g], axis=0
        )
        wide = on_diagonal(d_scores[g * length : (g + 1) * length], length)
        grad_first = jnp.dot(wide, second, preferred_element_type=jnp.float32)
        for q, e in enumerate(pairs_of_g):
            put_rows(by_first, e, length, pairs, grad_first[q * length : (q + 1) * length])


def pair_gradients(length, first_ref, place_ref, pool, received, laid, d_scores, by_second):
    pairs = first_ref.shape[1]
    across = LANES // length
    groups = pairs // across
    width = pool.shape[2]
    scale = 1.0 / (width * SOFTMAX_COOLING)
    together = groups

    side = (LANES, LANES)
    row_block = lax.div(lax.broadcasted_iota(jnp.int32, side, 0), length)
    lane_block = lax.div(lax.broadcasted_iota(jnp.int32, side, 1), length)
    diagonal = row_block == lane_block
    ones = jnp.where(diagonal, 1.0, 0.0).astype(jnp.bfloat16)
    ones = jnp.concatenate([ones, ones], axis=0)
    narrow = lax.div(lax.broadcasted_iota(jnp.int32, (length, LANES), 1), length)

    def block_sums(values):
        high = values.astype(jnp.bfloat16)
        low = (values - high.astype(jnp.float32)).astype(jnp.bfloat16)
        return jnp.dot(
            jnp.concatenate([high, low], axis=1), ones, preferred_element_type=jnp.float32
        )

    def step(chunk, carry):
        firsts, seconds, scores, incoming = [], [], [], []
        for n in range(together):
            g = chunk * together + n
            pairs_of_g = [q * groups + g for q in range(across)]
            firsts.append(jnp.concatenate([pool[first_ref[0, e]] for e in pairs_of_g], axis=0))
            seconds.append(
                jnp.concatenate(
                    [received[place_ref[0, e], place_ref[1, e]] for e in pairs_of_g], axis=0
                )
            )
            full = lax.dot_general(
                firsts[n],
                seconds[n],
                (((1,), (1,)), ((), ())),
                preferred_element_type=jnp.float32,
            )
            packed = full[:length]
            for q in range(1, across):
                packed = jnp.where(narrow == q, full[q * length : (q + 1) * length], packed)
            scores.append(packed)
            incoming.append(laid[pl.ds(g, length, stride=spread(groups)), :])
        shape = (together, length, LANES)
        expo = jnp.exp(jnp.concatenate(scores, axis=0) * scale)
        gradient = jnp.concatenate(incoming, axis=0)
        rows = expo / block_sums(expo)
        expo = expo.reshape(shape)
        cols = (expo / jnp.sum(expo, axis=1, keepdims=True)).reshape(rows.shape)
        both = gradient * rows * cols
        over_second = block_sums(both)
        over_first = jnp.sum(both.reshape(shape), axis=1, keepdims=True)
        part = (cols.reshape(shape) * over_first).reshape(rows.shape)
        d_scaled = ((2.0 * both - rows * over_second - part) * scale).astype(jnp.bfloat16)
        at = pl.multiple_of(chunk * (together * length), together * length)
        d_scores[pl.ds(at, together * length)] = d_scaled
        for n in range(together):
            wide = on_diagonal(d_scaled[n * length : (n + 1) * length], length)
            grad_second = lax.dot_general(
                wide, firsts[n], (((0,), (0,)), ((), ())), preferred_element_type=jnp.float32
            )
            for q in range(across):
                part = slice(q * length, (q + 1) * length)
                pair = q * groups + chunk * together + n
                put_rows(by_second, pair, length, pairs, grad_second[part])
        return carry

    lax.fori_loop(0, groups // together, step, 0)


def add_up(length, image_of_pair, by_pair, total, rounded):
    pairs = image_of_pair.shape[1]
    far = spread(length)
    halves, count = total.shape[0], total.shape[1] // far
    image = lax.broadcasted_iota(jnp.int32, (count, pairs), 0)
    chosen = jnp.where(image == image_of_pair[...], 1.0, 0.0).astype(jnp.bfloat16)
    together = length

    def step(chunk, carry):
        for n in range(together):
            i = chunk * together + n
            rows_of_i = pl.ds(pl.multiple_of(i * spread(pairs), 8), pairs)
            rows_of_i = [by_pair[h, rows_of_i].astype(jnp.bfloat16) for h in range(halves)]
            sums = jnp.dot(
                chosen, jnp.concatenate(rows_of_i, axis=1), preferred_element_type=jnp.float32
            )
            for h in range(halves):
                lanes = slice(h * LANES, (h + 1) * LANES)
                total[h, pl.ds(i, count, stride=far), :] = sums[:, lanes]
        return carry

    lax.fori_loop(0, length // together, step, 0)
    images = rounded.shape[1] // length
    for n in range(count):
        rows_of_image = slice(n % images * length, (n % images + 1) * length)
        for h in range(halves):
            rounded[n // images, rows_of_image, h * LANES : (h + 1) * LANES] = total[
                h, n * far : n * far + length
            ].astype(jnp.bfloat16)


def give_back(
    here,
    steps_y,
    steps_z,
    images,
    length,
    sum_pool,
    slots,
    pool,
    pick_rows,
    feature,
    arrived,
    choosers,
    y_in,
    y_out,
    z_in,
    z_out,
    y_send,
    y_recv,
    z_send,
    z_recv,
    x_send,
    x_recv,
):
    ring_y, ring_z, peers = here.ring_y, here.ring_z, here.peers
    rows, width = feature.shape
    half_y, half_z = ring_y // 2, ring_z // 2
    own = rows_at(here.s, length)
    plan = batches(ring_y)
    y_copies, z_copies, x_copies = {}, {}, {}

    def part_of(distance, way, half):
        return pl.ds(way * (rows // 2), rows // 2) if distance == half else pl.ds(0, rows)

    def send_z(distance):
        hop = distance - steps_z[distance]
        for way, turn in enumerate((1, -1)):
            part = part_of(distance, way, half_z)
            if distance in steps_z.values():
                source = z_out.at[way, distance - 1, part]
            else:
                source = pool.at[here.z_at(turn * distance), part]
            z_copies[distance, way] = send(
                source,
                z_in.at[way, distance - 1, part],
                z_send.at[way, distance - 1],
                z_recv.at[way, distance - 1],
                here.along_z(turn * hop),
            )

    def send_y(distance):
        hop = distance - steps_y[distance]
        for way, turn in enumerate((1, -1)):
            part = part_of(distance, way, half_y)
            y_copies[distance, way] = send(
                y_out.at[way, distance - 1, part],
                y_in.at[way, distance - 1, part],
                y_send.at[way, distance - 1],
                y_recv.at[way, distance - 1],
                here.along_y(turn * hop),
            )

    for distance in range(half_y, -1, -1):
        place, count = plan[distance]
        x_copies[distance] = [
            send(
                slots.at[pl.ds(place, count), rows_at(here.s_at(turn), length)],
                arrived.at[pl.ds(place, count), own],
                x_send.at[distance, turn - 1],
                x_recv.at[distance, turn - 1],
                here.across(turn),
            )
            for turn in range(1, peers)
        ]
    sum_pool()
    for distance in range(half_z, 0, -1):
        if distance not in steps_z.values():
            send_z(distance)
    for at in range(ring_y):
        arrived[at, own] = slots[at, own]
        choosers[at] = chooser(pick_rows[at, :1], images, length)

    def summed(place):
        return jnp.dot(choosers[place], arrived[place], preferred_element_type=jnp.float32)

    def wait_x(distance):
        for copy in x_copies[distance]:
            copy.wait_recv()

    def joined(total, ins, way, distance, half):
        if distance < half:
            return total + ins[way, distance - 1].astype(jnp.float32)
        low = way * (rows // 2)
        added = ins[way, distance - 1, low : low + rows // 2].astype(jnp.float32)
        added = added + total[low : low + rows // 2]
        rest = total[rows // 2 :] if way == 0 else total[: rows // 2]
        return jnp.concatenate([added, rest] if way == 0 else [rest, added], axis=0)

    def collect(total, way, distance, steps, copies, ins, half):
        for farther in sorted(steps, reverse=True):
            if steps[farther] == distance:
                copies[farther, way].wait_recv()
                total = joined(total, ins, way, farther, half)
        return total

    along_z = (steps_z, z_copies, z_in, half_z)
    along_y = (steps_y, y_copies, y_in, half_y)
    for distance in range(max(half_y, half_z), 0, -1):
        if distance <= half_y:
            wait_x(distance)
            for way, turn in enumerate((1, -1)):
                if distance < half_y or way == 0:
                    mine = summed(place_of(turn * distance, ring_y))
                total = collect(mine, way, distance, *along_y)
                y_out[way, distance - 1] = total.astype(jnp.bfloat16)
            send_y(distance)
        if distance <= half_z and distance in steps_z.values():
            for way, turn in enumerate((1, -1)):
                mine = pool[here.z_at(turn * distance)].astype(jnp.float32)
                total = collect(mine, way, distance, *along_z)
                z_out[way, distance - 1] = total.astype(jnp.bfloat16)
            send_z(distance)
    wait_x(0)
    gradient = summed(0) + pool[here.z].astype(jnp.float32)
    projected = feature[...]
    mean_square = jnp.mean(projected * projected, axis=-1, keepdims=True)
    inv_rms = lax.rsqrt(mean_square + EPSILON)
    normed = projected * inv_rms
    for way in range(2):
        gradient = collect(gradient, way, 0, *along_z)
        gradient = collect(gradient, way, 0, *along_y)
    mean = jnp.mean(gradient * normed, axis=-1, keepdims=True)
    for copy in [*y_copies.values(), *z_copies.values(), *sum(x_copies.values(), [])]:
        copy.wait_send()
    return (inv_rms * (gradient - normed * mean)).astype(jnp.bfloat16)


def kernel(grid, ring_z, steps_y, steps_z, images, length, *refs):
    arguments, (feature_grad, *scratch) = refs[:6], refs[6:]
    gathered, fetched, moved, sems = scratch[:9], scratch[9:17], scratch[17:30], scratch[30:]
    pool_images, received, laid, first_ref, firsts, place_ref, places, pick_rows, feature = gathered
    d_scores, by_first, by_second, pool_total, slot_total, slots, pool, *rings = moved
    here = Where(grid, ring_z)
    common = (here, steps_y, steps_z, images, length)
    gather(*common, arguments, *gathered, *fetched, *sems[:7])
    pair_gradients(length, first_ref, place_ref, pool_images, received, laid, d_scores, by_second)
    add_up(length, places, by_second, slot_total, slots)

    def sum_pool():
        first_gradients(length, place_ref, received, d_scores, by_first)
        add_up(length, firsts, by_first, pool_total, pool)

    feature_grad[...] = give_back(
        *common,
        sum_pool,
        slots,
        pool,
        pick_rows,
        feature,
        *rings,
        *sems[7:],
    )


def ring_semaphores(half_y, half_z, peers):
    dma = pltpu.SemaphoreType.DMA
    pairs = [(2, half_y), (2, half_z), (half_y + 1, peers - 1)]
    return [dma(shape) for shape in pairs for _ in range(2)]


def local(
    grid,
    ring_z,
    steps_y,
    steps_z,
    tokens,
    proj_weight,
    match_grad,
    edge_first,
    pair_second_image,
    send_pick,
):
    images, length, width = tokens.shape
    rows = images * length
    pairs = edge_first.shape[0]
    ring_y, peers = grid[1], grid[0] * grid[2]
    half_y, half_z = ring_y // 2, ring_z // 2
    layout = (grid, ring_z, steps_y, steps_z, images, length)
    bf16, f32 = jnp.bfloat16, jnp.float32

    block = (ring_y, peers * length, width)
    feature_grad = pl.pallas_call(
        functools.partial(kernel, *layout),
        out_shape=jax.ShapeDtypeStruct((rows, width), bf16),
        in_specs=[pl.BlockSpec(memory_space=pltpu.HBM)] * 6,
        out_specs=pl.BlockSpec(memory_space=pltpu.VMEM),
        scratch_shapes=[
            pltpu.VMEM((ring_z * images, length, width), bf16),
            pltpu.VMEM((ring_y, peers, length, width), bf16),
            pltpu.VMEM((length * spread(pairs * length // LANES), LANES), f32),
            pltpu.SMEM((1, pairs), jnp.int32),
            pltpu.VMEM((1, pairs), jnp.int32),
            pltpu.SMEM((2, pairs), jnp.int32),
            pltpu.VMEM((1, pairs), jnp.int32),
            pltpu.VMEM((ring_y, 8, peers * length), f32),
            pltpu.VMEM((rows, width), f32),
            pltpu.SMEM((send_pick.shape[0],), jnp.int32),
            pltpu.SMEM((1, pairs), jnp.int32),
            pltpu.VMEM((rows, width), bf16),
            pltpu.VMEM(proj_weight.shape, bf16),
            pltpu.VMEM(match_grad.shape, bf16),
            pltpu.VMEM((1, pairs), jnp.int32),
            pltpu.VMEM((ring_y, rows + 16, width), bf16),
            pltpu.VMEM(block, bf16),
            pltpu.VMEM((pairs * length * length // LANES, LANES), bf16),
            pltpu.VMEM((width // LANES, length * spread(pairs), LANES), f32),
            pltpu.VMEM((width // LANES, length * spread(pairs), LANES), f32),
            pltpu.VMEM((width // LANES, ring_z * images * spread(length), LANES), f32),
            pltpu.VMEM((width // LANES, ring_y * peers * spread(length), LANES), f32),
            pltpu.VMEM(block, bf16),
            pltpu.VMEM((ring_z, rows, width), bf16),
            pltpu.VMEM(block, bf16),
            pltpu.VMEM((ring_y, rows, peers * length), bf16),
            pltpu.VMEM((2, half_y, rows, width), bf16),
            pltpu.VMEM((2, half_y, rows, width), bf16),
            pltpu.VMEM((2, half_z, rows, width), bf16),
            pltpu.VMEM((2, half_z, rows, width), bf16),
            pltpu.SemaphoreType.DMA((8,)),
            *ring_semaphores(half_y, half_z, peers),
            *ring_semaphores(half_y, half_z, peers),
        ],
        compiler_params=pltpu.CompilerParams(
            collective_id=0, has_side_effects=True, vmem_limit_bytes=VMEM_LIMIT
        ),
        name="feature_gradients",
    )(
        *(
            pltpu.with_memory_space_constraint(argument, pltpu.HBM)
            for argument in (
                send_pick,
                tokens.reshape(rows, width),
                proj_weight,
                match_grad,
                edge_first.reshape(1, pairs),
                pair_second_image.reshape(1, pairs),
            )
        )
    )
    token_grad = lax.dot_general(
        feature_grad, proj_weight, (((1,), (1,)), ((), ())), preferred_element_type=f32
    )
    return token_grad.astype(bf16).reshape(images, length, width)


def solution(mesh, grid=GRID, steps_y=STEPS_Y, steps_z=STEPS_Z):
    placed = (
        P(("grp", "sub"), None, None),
        P(),
        P(("grp", "sub"), None),
        P(("grp", "sub")),
        P(("grp", "sub")),
        P(("grp", "sub")),
    )
    return jax.shard_map(
        functools.partial(local, grid, mesh.shape["sub"], steps_y, steps_z),
        mesh=mesh,
        in_specs=placed,
        out_specs=P(("grp", "sub"), None, None),
        check_vma=False,
    )
```

```python
import functools

import jax
import jax.numpy as jnp
from jax import lax
from jax.experimental import pallas as pl
from jax.experimental.pallas import tpu as pltpu
from jax.sharding import PartitionSpec as P

EPSILON = 1e-05
SOFTMAX_COOLING = 0.1
MESH = pl.DeviceIdType.MESH
LANES = 128
VMEM_LIMIT = 40 * 1024 * 1024
GRID = (4, 8, 2)
STEPS_Y = {1: 0, 2: 0, 3: 1, 4: 2}
STEPS_Z = {2: 0, 1: 0, 4: 2, 3: 2, 6: 4, 5: 4}
ARRIVALS = (
    ("y", 1),
    ("z", 2),
    ("y", 2),
    ("z", 1),
    ("z", 4),
    ("y", 3),
    ("y", 4),
    ("z", 3),
    ("z", 6),
    ("z", 5),
)


def place_of(offset, ring):
    offset %= ring
    return 0 if offset == 0 else 2 * offset - 1 if 2 * offset <= ring else 2 * (ring - offset)


class Where:
    def __init__(self, grid, ring_z):
        _, self.ring_y, cores = grid
        self.cores, self.ring_z, self.peers = cores, ring_z, grid[0] * cores
        grp = lax.axis_index("grp")
        self.z = lax.axis_index("sub")
        self.y = lax.rem(lax.div(grp, cores), self.ring_y)
        self.s = lax.div(grp, cores * self.ring_y) * cores + lax.rem(grp, cores)

    def group(self, s, y):
        return (lax.div(s, self.cores) * self.ring_y + y) * self.cores + lax.rem(s, self.cores)

    def along_y(self, step):
        return {"grp": self.group(self.s, lax.rem(self.y + step + self.ring_y, self.ring_y))}

    def z_at(self, step):
        return lax.rem(self.z + step + self.ring_z, self.ring_z)

    def along_z(self, step):
        return {"sub": self.z_at(step)}

    def s_at(self, turn):
        return lax.rem(self.s + turn, self.peers)

    def across(self, turn):
        return {"grp": self.group(self.s_at(turn), self.y)}

    def greet(self, steps_y, steps_z):
        barrier = pltpu.get_barrier_semaphore()
        others = []
        for hop in sorted({distance - before for distance, before in steps_y.items()}):
            others += [self.along_y(hop), self.along_y(-hop)]
        for hop in sorted({distance - before for distance, before in steps_z.items()}):
            others += [self.along_z(hop), self.along_z(-hop)]
        others += [self.across(turn) for turn in range(1, self.peers)]
        for other in others:
            pl.semaphore_signal(barrier, inc=1, device_id=other, device_id_type=MESH)
        return lambda: pl.semaphore_wait(barrier, len(others))


def send(src, dst, send_sem, recv_sem, device):
    copy = pltpu.make_async_remote_copy(
        src_ref=src,
        dst_ref=dst,
        send_sem=send_sem,
        recv_sem=recv_sem,
        device_id=device,
        device_id_type=MESH,
    )
    copy.start()
    return copy


def batches(ring):
    half = ring // 2
    return [(0, 1)] + [(2 * d - 1, 2) for d in range(1, half)] + [(ring - 1, 1)]


def spread(count):
    return (count // 8 | 1) * 8


def rows_at(index, count):
    return pl.ds(pl.multiple_of(index * count, count), count)


def chooser(pick_row, images, length):
    shape = (images * length, pick_row.shape[1])
    row = lax.broadcasted_iota(jnp.int32, shape, 0)
    column = lax.broadcasted_iota(jnp.int32, shape, 1)
    image = lax.div(row, length).astype(jnp.float32)
    same = lax.rem(row, length) == lax.rem(column, length)
    return jnp.where(same & (image == pick_row), 1.0, 0.0).astype(jnp.bfloat16)


def gather(
    here,
    steps_y,
    steps_z,
    images,
    length,
    arguments,
    pool,
    received,
    laid,
    first_ref,
    firsts,
    place_ref,
    places,
    pick_rows,
    feature,
    picks,
    second_ref,
    tokens,
    weight,
    grads,
    seconds,
    blocks,
    stage,
    fetch_sem,
    y_send,
    y_recv,
    z_send,
    z_recv,
    x_send,
    x_recv,
):
    ring_y, ring_z, peers = here.ring_y, here.ring_z, here.peers
    rows, width = tokens.shape
    block_rows = blocks.shape[1]
    picks_arg, tokens_arg, weight_arg, grads_arg, firsts_arg, seconds_arg = arguments
    met = here.greet(steps_y, steps_z)
    fetches = [
        pltpu.make_async_copy(src, dst, fetch_sem.at[n])
        for n, (src, dst) in enumerate(
            (
                (tokens_arg, tokens),
                (weight_arg, weight),
                (picks_arg, picks),
                (seconds_arg, seconds),
                (seconds_arg, second_ref),
                (firsts_arg, firsts),
                (firsts_arg, first_ref),
                (grads_arg, grads),
            )
        )
    ]
    for fetch in fetches:
        fetch.start()
    for fetch in fetches[:3]:
        fetch.wait()
    projected = jnp.dot(tokens[...], weight[...], preferred_element_type=jnp.float32)
    feature[...] = projected
    mean_square = jnp.mean(projected * projected, axis=-1, keepdims=True)
    normed = (projected * lax.rsqrt(mean_square + EPSILON)).astype(jnp.bfloat16)
    blocks[0, :rows] = normed
    for n in range(images):
        pool[here.z * images + n] = normed[n * length : (n + 1) * length]
    tail = (block_rows - rows, peers * length)
    tail_row = lax.broadcasted_iota(jnp.int32, tail, 0)
    tail_peer = lax.div(lax.broadcasted_iota(jnp.int32, tail, 1), length)
    table = jnp.zeros(tail, jnp.int32)
    for y in range(ring_y):
        for s in range(peers):
            slot = (s // here.cores * ring_y + y) * here.cores + s % here.cores
            table = jnp.where((tail_row == y) & (tail_peer == s), picks[slot], table)
    blocks[0, rows:] = table.astype(jnp.float32).astype(jnp.bfloat16)
    met()

    half_y, half_z = ring_y // 2, ring_z // 2
    y_copies, z_copies, x_copies = {}, {}, []

    def forward_y(source):
        for distance, before in steps_y.items():
            if before != source:
                continue
            for way, turn in enumerate((1, -1)):
                part = pl.ds(0, block_rows)
                if distance == half_y:
                    part = pl.ds(0, rows // 2) if way == 0 else pl.ds(rows // 2, block_rows - rows // 2)
                y_copies[distance, way] = send(
                    blocks.at[place_of(-turn * before, ring_y), part],
                    blocks.at[place_of(-turn * distance, ring_y), part],
                    y_send.at[way, distance - 1],
                    y_recv.at[way, distance - 1],
                    here.along_y(turn * (distance - before)),
                )

    def forward_z(source):
        for distance, before in steps_z.items():
            if before != source:
                continue
            for way, turn in enumerate((1, -1)):
                first = here.z_at(-turn * before) * images
                part = pl.ds(first, images)
                if distance == half_z:
                    part = pl.ds(first + way * (images // 2), images // 2)
                z_copies[distance, way] = send(
                    pool.at[part],
                    pool.at[part],
                    z_send.at[way, distance - 1],
                    z_recv.at[way, distance - 1],
                    here.along_z(turn * (distance - before)),
                )

    own = rows_at(here.s, length)

    def choose(batch, place, count):
        for at in range(place, place + count):
            rows_of_y = blocks[at, rows:].astype(jnp.float32)
            mine = jnp.sum(jnp.where(tail_row == here.y, rows_of_y, 0.0), axis=0, keepdims=True)
            pick_rows[at] = jnp.broadcast_to(mine, pick_rows.shape[1:])
            stage[at] = lax.dot_general(
                chooser(mine, images, length),
                blocks[at, :rows],
                (((0,), (0,)), ((), ())),
                preferred_element_type=jnp.float32,
            ).astype(jnp.bfloat16)
        for turn in range(1, peers):
            x_copies.append(
                send(
                    stage.at[pl.ds(place, count), rows_at(here.s_at(turn), length)],
                    received.at[pl.ds(place, count), here.s],
                    x_send.at[batch, turn - 1],
                    x_recv.at[batch, turn - 1],
                    here.across(turn),
                )
            )
        for at in range(place, place + count):
            received[at, here.s] = stage[at, own]

    forward_y(0)
    forward_z(0)
    plan = batches(ring_y)
    choose(0, *plan[0])
    for fetch in fetches[3:]:
        fetch.wait()

    def find(slot):
        offset = lax.rem(lax.rem(lax.div(slot, here.cores), ring_y) - here.y + ring_y, ring_y)
        near = jnp.where(2 * offset <= ring_y, 2 * offset - 1, 2 * (ring_y - offset))
        peer = lax.div(slot, here.cores * ring_y) * here.cores + lax.rem(slot, here.cores)
        return jnp.where(offset == 0, 0, near), peer

    def note(e, carry):
        place_ref[0, e], place_ref[1, e] = find(second_ref[0, e])
        return carry

    def find_all():
        place, peer = find(seconds[...])
        places[...] = place * peers + peer
        lax.fori_loop(0, second_ref.shape[1], note, 0)

    across = LANES // length
    groups = grads.shape[0] // across
    lane_block = lax.div(lax.broadcasted_iota(jnp.int32, (groups, LANES), 1), length)

    def lay(tile):
        wide = grads[:, tile * LANES : (tile + 1) * LANES].astype(jnp.float32)
        parts = [wide[q * groups : (q + 1) * groups] for q in range(across)]
        for r in range(across):
            total = None
            for q in range(across):
                shift = (q - r) % across * length
                moved = pltpu.roll(parts[q], shift, 1) if shift else parts[q]
                total = moved if total is None else jnp.where(lane_block == q, moved, total)
            i = tile * across + r
            laid[i * spread(groups) : i * spread(groups) + groups] = total

    tiles = grads.shape[1] // LANES
    todo = list(range(tiles))
    for axis, distance in ARRIVALS:
        if todo:
            lay(todo.pop(0))
        if axis == "y" and distance <= half_y:
            for way in range(2):
                y_copies[distance, way].wait_recv()
            forward_y(distance)
            choose(distance, *plan[distance])
            if distance == half_y:
                find_all()
        if axis == "z" and distance <= half_z:
            for way in range(2):
                z_copies[distance, way].wait_recv()
            forward_z(distance)
    for tile in todo:
        lay(tile)
    for copy in x_copies:
        copy.wait_recv()
    for copy in [*y_copies.values(), *z_copies.values(), *x_copies]:
        copy.wait_send()


def put_rows(by_pair, pair, length, pairs, values):
    for h in range(by_pair.shape[0]):
        by_pair[h, pl.ds(pair, length, stride=spread(pairs)), :] = values[
            :, h * LANES : (h + 1) * LANES
        ]


def on_diagonal(packed, length):
    side = (LANES, LANES)
    row_block = lax.div(lax.broadcasted_iota(jnp.int32, side, 0), length)
    lane_block = lax.div(lax.broadcasted_iota(jnp.int32, side, 1), length)
    wide = jnp.concatenate([packed] * (LANES // length), axis=0)
    return jnp.where(row_block == lane_block, wide, jnp.zeros_like(wide))


def first_gradients(length, place_ref, received, d_scores, by_first):
    pairs = place_ref.shape[1]
    across = LANES // length
    groups = pairs // across
    for g in range(groups):
        pairs_of_g = [q * groups + g for q in range(across)]
        second = jnp.concatenate(
            [received[place_ref[0, e], place_ref[1, e]] for e in pairs_of_g], axis=0
        )
        wide = on_diagonal(d_scores[g * length : (g + 1) * length], length)
        grad_first = jnp.dot(wide, second, preferred_element_type=jnp.float32)
        for q, e in enumerate(pairs_of_g):
            put_rows(by_first, e, length, pairs, grad_first[q * length : (q + 1) * length])


def pair_gradients(length, first_ref, place_ref, pool, received, laid, d_scores, by_second):
    pairs = first_ref.shape[1]
    across = LANES // length
    groups = pairs // across
    width = pool.shape[2]
    scale = 1.0 / (width * SOFTMAX_COOLING)
    together = groups

    side = (LANES, LANES)
    row_block = lax.div(lax.broadcasted_iota(jnp.int32, side, 0), length)
    lane_block = lax.div(lax.broadcasted_iota(jnp.int32, side, 1), length)
    diagonal = row_block == lane_block
    ones = jnp.where(diagonal, 1.0, 0.0).astype(jnp.bfloat16)
    ones = jnp.concatenate([ones, ones], axis=0)
    narrow = lax.div(lax.broadcasted_iota(jnp.int32, (length, LANES), 1), length)

    def block_sums(values):
        high = values.astype(jnp.bfloat16)
        low = (values - high.astype(jnp.float32)).astype(jnp.bfloat16)
        return jnp.dot(
            jnp.concatenate([high, low], axis=1), ones, preferred_element_type=jnp.float32
        )

    def step(chunk, carry):
        firsts, seconds, scores, incoming = [], [], [], []
        for n in range(together):
            g = chunk * together + n
            pairs_of_g = [q * groups + g for q in range(across)]
            firsts.append(jnp.concatenate([pool[first_ref[0, e]] for e in pairs_of_g], axis=0))
            seconds.append(
                jnp.concatenate(
                    [received[place_ref[0, e], place_ref[1, e]] for e in pairs_of_g], axis=0
                )
            )
            full = lax.dot_general(
                firsts[n],
                seconds[n],
                (((1,), (1,)), ((), ())),
                preferred_element_type=jnp.float32,
            )
            packed = full[:length]
            for q in range(1, across):
                packed = jnp.where(narrow == q, full[q * length : (q + 1) * length], packed)
            scores.append(packed)
            incoming.append(laid[pl.ds(g, length, stride=spread(groups)), :])
        shape = (together, length, LANES)
        expo = jnp.exp(jnp.concatenate(scores, axis=0) * scale)
        gradient = jnp.concatenate(incoming, axis=0)
        rows = expo / block_sums(expo)
        expo = expo.reshape(shape)
        cols = (expo / jnp.sum(expo, axis=1, keepdims=True)).reshape(rows.shape)
        both = gradient * rows * cols
        over_second = block_sums(both)
        over_first = jnp.sum(both.reshape(shape), axis=1, keepdims=True)
        part = (cols.reshape(shape) * over_first).reshape(rows.shape)
        d_scaled = ((2.0 * both - rows * over_second - part) * scale).astype(jnp.bfloat16)
        at = pl.multiple_of(chunk * (together * length), together * length)
        d_scores[pl.ds(at, together * length)] = d_scaled
        for n in range(together):
            wide = on_diagonal(d_scaled[n * length : (n + 1) * length], length)
            grad_second = lax.dot_general(
                wide, firsts[n], (((0,), (0,)), ((), ())), preferred_element_type=jnp.float32
            )
            for q in range(across):
                part = slice(q * length, (q + 1) * length)
                pair = q * groups + chunk * together + n
                put_rows(by_second, pair, length, pairs, grad_second[part])
        return carry

    lax.fori_loop(0, groups // together, step, 0)


def add_up(length, image_of_pair, by_pair, total, rounded):
    pairs = image_of_pair.shape[1]
    far = spread(length)
    halves, count = total.shape[0], total.shape[1] // far
    image = lax.broadcasted_iota(jnp.int32, (count, pairs), 0)
    chosen = jnp.where(image == image_of_pair[...], 1.0, 0.0).astype(jnp.bfloat16)
    together = length

    def step(chunk, carry):
        for n in range(together):
            i = chunk * together + n
            rows_of_i = pl.ds(pl.multiple_of(i * spread(pairs), 8), pairs)
            rows_of_i = [by_pair[h, rows_of_i].astype(jnp.bfloat16) for h in range(halves)]
            sums = jnp.dot(
                chosen, jnp.concatenate(rows_of_i, axis=1), preferred_element_type=jnp.float32
            )
            for h in range(halves):
                lanes = slice(h * LANES, (h + 1) * LANES)
                total[h, pl.ds(i, count, stride=far), :] = sums[:, lanes]
        return carry

    lax.fori_loop(0, length // together, step, 0)
    images = rounded.shape[1] // length
    for n in range(count):
        rows_of_image = slice(n % images * length, (n % images + 1) * length)
        for h in range(halves):
            rounded[n // images, rows_of_image, h * LANES : (h + 1) * LANES] = total[
                h, n * far : n * far + length
            ].astype(jnp.bfloat16)


def give_back(
    here,
    steps_y,
    steps_z,
    images,
    length,
    sum_pool,
    slots,
    pool,
    pick_rows,
    feature,
    arrived,
    choosers,
    y_in,
    y_out,
    z_in,
    z_out,
    y_send,
    y_recv,
    z_send,
    z_recv,
    x_send,
    x_recv,
):
    ring_y, ring_z, peers = here.ring_y, here.ring_z, here.peers
    rows, width = feature.shape
    half_y, half_z = ring_y // 2, ring_z // 2
    own = rows_at(here.s, length)
    plan = batches(ring_y)
    y_copies, z_copies, x_copies = {}, {}, {}

    def part_of(distance, way, half):
        return pl.ds(way * (rows // 2), rows // 2) if distance == half else pl.ds(0, rows)

    def send_z(distance):
        hop = distance - steps_z[distance]
        for way, turn in enumerate((1, -1)):
            part = part_of(distance, way, half_z)
            if distance in steps_z.values():
                source = z_out.at[way, distance - 1, part]
            else:
                source = pool.at[here.z_at(turn * distance), part]
            z_copies[distance, way] = send(
                source,
                z_in.at[way, distance - 1, part],
                z_send.at[way, distance - 1],
                z_recv.at[way, distance - 1],
                here.along_z(turn * hop),
            )

    def send_y(distance):
        hop = distance - steps_y[distance]
        for way, turn in enumerate((1, -1)):
            part = part_of(distance, way, half_y)
            y_copies[distance, way] = send(
                y_out.at[way, distance - 1, part],
                y_in.at[way, distance - 1, part],
                y_send.at[way, distance - 1],
                y_recv.at[way, distance - 1],
                here.along_y(turn * hop),
            )

    for distance in range(half_y, -1, -1):
        place, count = plan[distance]
        x_copies[distance] = [
            send(
                slots.at[pl.ds(place, count), rows_at(here.s_at(turn), length)],
                arrived.at[pl.ds(place, count), own],
                x_send.at[distance, turn - 1],
                x_recv.at[distance, turn - 1],
                here.across(turn),
            )
            for turn in range(1, peers)
        ]
    sum_pool()
    for distance in range(half_z, 0, -1):
        if distance not in steps_z.values():
            send_z(distance)
    for at in range(ring_y):
        arrived[at, own] = slots[at, own]
        choosers[at] = chooser(pick_rows[at, :1], images, length)

    def summed(place):
        return jnp.dot(choosers[place], arrived[place], preferred_element_type=jnp.float32)

    def wait_x(distance):
        for copy in x_copies[distance]:
            copy.wait_recv()

    def joined(total, ins, way, distance, half):
        if distance < half:
            return total + ins[way, distance - 1].astype(jnp.float32)
        low = way * (rows // 2)
        added = ins[way, distance - 1, low : low + rows // 2].astype(jnp.float32)
        added = added + total[low : low + rows // 2]
        rest = total[rows // 2 :] if way == 0 else total[: rows // 2]
        return jnp.concatenate([added, rest] if way == 0 else [rest, added], axis=0)

    def collect(total, way, distance, steps, copies, ins, half):
        for farther in sorted(steps, reverse=True):
            if steps[farther] == distance:
                copies[farther, way].wait_recv()
                total = joined(total, ins, way, farther, half)
        return total

    along_z = (steps_z, z_copies, z_in, half_z)
    along_y = (steps_y, y_copies, y_in, half_y)
    for distance in range(max(half_y, half_z), 0, -1):
        if distance <= half_y:
            wait_x(distance)
            for way, turn in enumerate((1, -1)):
                if distance < half_y or way == 0:
                    mine = summed(place_of(turn * distance, ring_y))
                total = collect(mine, way, distance, *along_y)
                y_out[way, distance - 1] = total.astype(jnp.bfloat16)
            send_y(distance)
        if distance <= half_z and distance in steps_z.values():
            for way, turn in enumerate((1, -1)):
                mine = pool[here.z_at(turn * distance)].astype(jnp.float32)
                total = collect(mine, way, distance, *along_z)
                z_out[way, distance - 1] = total.astype(jnp.bfloat16)
            send_z(distance)
    wait_x(0)
    gradient = summed(0) + pool[here.z].astype(jnp.float32)
    projected = feature[...]
    mean_square = jnp.mean(projected * projected, axis=-1, keepdims=True)
    inv_rms = lax.rsqrt(mean_square + EPSILON)
    normed = projected * inv_rms
    for way in range(2):
        gradient = collect(gradient, way, 0, *along_z)
        gradient = collect(gradient, way, 0, *along_y)
    mean = jnp.mean(gradient * normed, axis=-1, keepdims=True)
    for copy in [*y_copies.values(), *z_copies.values(), *sum(x_copies.values(), [])]:
        copy.wait_send()
    return (inv_rms * (gradient - normed * mean)).astype(jnp.bfloat16)


def kernel(grid, ring_z, steps_y, steps_z, images, length, *refs):
    arguments, (feature_grad, *scratch) = refs[:6], refs[6:]
    gathered, fetched, moved, sems = scratch[:9], scratch[9:17], scratch[17:30], scratch[30:]
    pool_images, received, laid, first_ref, firsts, place_ref, places, pick_rows, feature = gathered
    d_scores, by_first, by_second, pool_total, slot_total, slots, pool, *rings = moved
    here = Where(grid, ring_z)
    common = (here, steps_y, steps_z, images, length)
    gather(*common, arguments, *gathered, *fetched, *sems[:7])
    pair_gradients(length, first_ref, place_ref, pool_images, received, laid, d_scores, by_second)
    add_up(length, places, by_second, slot_total, slots)

    def sum_pool():
        first_gradients(length, place_ref, received, d_scores, by_first)
        add_up(length, firsts, by_first, pool_total, pool)

    feature_grad[...] = give_back(
        *common,
        sum_pool,
        slots,
        pool,
        pick_rows,
        feature,
        *rings,
        *sems[7:],
    )


def ring_semaphores(half_y, half_z, peers):
    dma = pltpu.SemaphoreType.DMA
    pairs = [(2, half_y), (2, half_z), (half_y + 1, peers - 1)]
    return [dma(shape) for shape in pairs for _ in range(2)]


def local(
    grid,
    ring_z,
    steps_y,
    steps_z,
    tokens,
    proj_weight,
    match_grad,
    edge_first,
    pair_second_image,
    send_pick,
):
    images, length, width = tokens.shape
    rows = images * length
    pairs = edge_first.shape[0]
    ring_y, peers = grid[1], grid[0] * grid[2]
    half_y, half_z = ring_y // 2, ring_z // 2
    layout = (grid, ring_z, steps_y, steps_z, images, length)
    bf16, f32 = jnp.bfloat16, jnp.float32

    block = (ring_y, peers * length, width)
    feature_grad = pl.pallas_call(
        functools.partial(kernel, *layout),
        out_shape=jax.ShapeDtypeStruct((rows, width), bf16),
        in_specs=[pl.BlockSpec(memory_space=pltpu.HBM)] * 6,
        out_specs=pl.BlockSpec(memory_space=pltpu.VMEM),
        scratch_shapes=[
            pltpu.VMEM((ring_z * images, length, width), bf16),
            pltpu.VMEM((ring_y, peers, length, width), bf16),
            pltpu.VMEM((length * spread(pairs * length // LANES), LANES), f32),
            pltpu.SMEM((1, pairs), jnp.int32),
            pltpu.VMEM((1, pairs), jnp.int32),
            pltpu.SMEM((2, pairs), jnp.int32),
            pltpu.VMEM((1, pairs), jnp.int32),
            pltpu.VMEM((ring_y, 8, peers * length), f32),
            pltpu.VMEM((rows, width), f32),
            pltpu.SMEM((send_pick.shape[0],), jnp.int32),
            pltpu.SMEM((1, pairs), jnp.int32),
            pltpu.VMEM((rows, width), bf16),
            pltpu.VMEM(proj_weight.shape, bf16),
            pltpu.VMEM(match_grad.shape, bf16),
            pltpu.VMEM((1, pairs), jnp.int32),
            pltpu.VMEM((ring_y, rows + 16, width), bf16),
            pltpu.VMEM(block, bf16),
            pltpu.VMEM((pairs * length * length // LANES, LANES), bf16),
            pltpu.VMEM((width // LANES, length * spread(pairs), LANES), f32),
            pltpu.VMEM((width // LANES, length * spread(pairs), LANES), f32),
            pltpu.VMEM((width // LANES, ring_z * images * spread(length), LANES), f32),
            pltpu.VMEM((width // LANES, ring_y * peers * spread(length), LANES), f32),
            pltpu.VMEM(block, bf16),
            pltpu.VMEM((ring_z, rows, width), bf16),
            pltpu.VMEM(block, bf16),
            pltpu.VMEM((ring_y, rows, peers * length), bf16),
            pltpu.VMEM((2, half_y, rows, width), bf16),
            pltpu.VMEM((2, half_y, rows, width), bf16),
            pltpu.VMEM((2, half_z, rows, width), bf16),
            pltpu.VMEM((2, half_z, rows, width), bf16),
            pltpu.SemaphoreType.DMA((8,)),
            *ring_semaphores(half_y, half_z, peers),
            *ring_semaphores(half_y, half_z, peers),
        ],
        compiler_params=pltpu.CompilerParams(
            collective_id=0, has_side_effects=True, vmem_limit_bytes=VMEM_LIMIT
        ),
        name="feature_gradients",
    )(
        *(
            pltpu.with_memory_space_constraint(argument, pltpu.HBM)
            for argument in (
                send_pick,
                tokens.reshape(rows, width),
                proj_weight,
                match_grad,
                edge_first.reshape(1, pairs),
                pair_second_image.reshape(1, pairs),
            )
        )
    )
    token_grad = lax.dot_general(
        feature_grad, proj_weight, (((1,), (1,)), ((), ())), preferred_element_type=f32
    )
    return token_grad.astype(bf16).reshape(images, length, width)


def solution(mesh, grid=GRID, steps_y=STEPS_Y, steps_z=STEPS_Z):
    placed = (
        P(("grp", "sub"), None, None),
        P(),
        P(("grp", "sub"), None),
        P(("grp", "sub")),
        P(("grp", "sub")),
        P(("grp", "sub")),
    )
    return jax.shard_map(
        functools.partial(local, grid, mesh.shape["sub"], steps_y, steps_z),
        mesh=mesh,
        in_specs=placed,
        out_specs=P(("grp", "sub"), None, None),
        check_vma=False,
    )
```
